256 devices in a mesh: blk: 32 (over x_lo, z, core), grp: 8 (over x_hi, y).
Axes of the slice: x: 4 (x_hi: 2, x_lo: 2; x = x_hi * 2 + x_lo), y: 4, z: 8, core: 2. Of those that a mesh axis runs over, the one named last changes fastest.
Arguments:
- spectra: bfloat16 [2, 128, 640, 4096], P(None, 'grp', None, 'blk'), may hold values from -6 to 6
- pattern: int32 [32, 32], replicated, may hold values from 0 to 1, as said below
- slot_of_pair: int32 [32, 32], replicated, may hold values from 0 to 7, as said below
Outputs:
- stacks: bfloat16 [8, 512, 4, 4096], P('grp', None, None, 'blk')
The draws below stay inside these ranges and needn't reach their ends.
Inputs may be any that keep to these rules, and one draw needn't show every extreme that they name: `pattern`: every block pairs with itself and with the blocks next to it; each column j holds at most 8 ones, and some column exactly 8. `slot_of_pair`: within a column j the pairs with pattern 1 have distinct slots; slots g * 1 to (g + 1) - 1 belong to owner g of the grp axis; in some column every slot is used. Entries where pattern is 0 carry no meaning.
All inputs are finite; a program needn't handle non-finite values.
Results may differ from the reference program's by a relative error of at most 0.0055.
Values may be sent and summed in bfloat16 or wider, within the bound.
A program may use at most 128 MiB of HBM per device.

```python
import math
import jax
import jax.numpy as jnp
from jax import lax

CB = 128
F = 640
LAGS = 512
VS = 4
WIN_DEV = 16
PAIRS_MAX = 8
BLOCKS = 32
CHANNELS = 4096
WINDOWS = 128
N_GRP = 8


def pair_layout(key):
    rows = jnp.arange(BLOCKS, dtype=jnp.int32)
    band = (jnp.abs(rows[:, None] - rows[None, :]) <= 1).astype(jnp.int32)
    band_count = jnp.sum(band, axis=0).astype(jnp.int32)
    room = (PAIRS_MAX - band_count).astype(jnp.int32)
    keys = jax.random.split(key, 5)
    first = jax.random.randint(keys[0], (BLOCKS,), 0, room + 1, dtype=jnp.int32)
    second = jax.random.randint(keys[1], (BLOCKS,), 0, room + 1, dtype=jnp.int32)
    extra = first * second // jnp.maximum(room, 1)
    heavy = jax.random.randint(keys[2], (), 0, BLOCKS, dtype=jnp.int32)
    extra = jnp.where(rows == heavy, room, extra).astype(jnp.int32)
    scores = jax.random.randint(keys[3], (BLOCKS, BLOCKS), 0, BLOCKS, dtype=jnp.int32) * BLOCKS + rows[:, None] + band * (BLOCKS * BLOCKS)
    ranks = jnp.argsort(jnp.argsort(scores, axis=0), axis=0).astype(jnp.int32)
    pattern = jnp.maximum(band, (ranks < extra[None, :]).astype(jnp.int32)).astype(jnp.int32)
    order = (jnp.cumsum(pattern, axis=0) - 1).astype(jnp.int32)
    order = jnp.clip(order, 0, PAIRS_MAX - 1)
    levels = jnp.arange(PAIRS_MAX, dtype=jnp.int32)
    perm_scores = jax.random.randint(keys[4], (PAIRS_MAX, BLOCKS), 0, PAIRS_MAX, dtype=jnp.int32) * PAIRS_MAX + levels[:, None]
    perms = jnp.argsort(perm_scores, axis=0).astype(jnp.int32)
    slots = jnp.take_along_axis(perms, order, axis=0).astype(jnp.int32)
    return (pattern, slots)


def draw_pattern(key, part):
    return pair_layout(key)[0]


def draw_slot_of_pair(key, part):
    return pair_layout(key)[1]


def block_levels(own_key, extent, shards, low, top_value):
    level = 1.0
    for position, parts in shards:
        steps = jax.random.uniform(jax.random.fold_in(jax.random.fold_in(own_key, 6), position), (parts,), jnp.float32, low / len(shards), top_value / len(shards))
        level = level * jnp.repeat(jnp.exp(steps), extent[position] // parts).reshape((-1,) + (1,) * (len(extent) - 1 - position))
    return level


def scatter_about(key, shape, scale, limit, pieces=(), kind=jnp.bfloat16):
    array = jax.random.normal(key, shape, jnp.float32) * scale
    if len(pieces) > 0:
        array = block_levels(key, shape, pieces, -0.22, 0.18) * array
    return jnp.clip(array, min=-limit, max=limit).astype(kind)


def setup_inputs(seed: int = 0) -> dict:
    streams_of = jax.random.split(jax.random.key(seed), 4)
    return {
        "spectra": scatter_about(streams_of[0], (2, WINDOWS, F, CHANNELS), 1.0, 6.0, ((1, 8), (3, 32))),
        "pattern": draw_pattern(jax.random.fold_in(streams_of[3], 71), 0),
        "slot_of_pair": draw_slot_of_pair(jax.random.fold_in(streams_of[3], 71), 0),
    }


def lag_table(freq_count, lag_count, windows, repeats):
    freq_bins = jnp.arange(freq_count, dtype=jnp.int32)
    shifts = jnp.arange(lag_count, dtype=jnp.int32) - lag_count // 2
    phases = shifts[:, None] * freq_bins[None, :] % (2 * freq_count)
    angles = math.pi / freq_count * phases.astype(jnp.float32)
    factor = 1.0 / math.sqrt(2.0 * windows * freq_count)
    rows = jnp.concatenate([jnp.cos(angles), -jnp.sin(angles)], axis=1) * factor
    return jnp.tile(rows, (1, repeats)).astype(jnp.bfloat16)

def cross_reference(sources, receivers):
    wide_sources = sources.astype(jnp.float32)
    wide_receivers = receivers.astype(jnp.float32)
    turned = jnp.stack([wide_sources[1], -wide_sources[0]])
    real_part = jnp.einsum('pgwsf,pgwfc->gfsc', wide_sources, wide_receivers)
    imag_part = jnp.einsum('pgwsf,pgwfc->gfsc', turned, wide_receivers)
    crossed = jnp.stack([real_part, imag_part], axis=1).astype(jnp.bfloat16)
    segments = crossed.shape[0]
    return crossed.reshape(segments * 2 * crossed.shape[2], crossed.shape[3] * crossed.shape[4])

def reference(spectra, pattern, slot_of_pair):
    transform = lag_table(F, LAGS, WIN_DEV * N_GRP, N_GRP)
    zero_index = jnp.zeros((), jnp.int32)

    def column_stacks(column):
        receivers = lax.dynamic_slice_in_dim(spectra, (column * CB).astype(jnp.int32), CB, 3).reshape(2, N_GRP, WIN_DEV, F, CB)
        running = jnp.cumsum(pattern[:, column]).astype(jnp.int32)

        def add_pair(number, buffer):
            found = jnp.sum((running <= number).astype(jnp.int32))
            source_block = jnp.minimum(found, BLOCKS - 1).astype(jnp.int32)
            present = number < running[-1]

            def compute(buffer):
                sources = lax.dynamic_slice_in_dim(spectra, (source_block * CB).astype(jnp.int32), VS, 3)
                sources = jnp.transpose(sources, (0, 1, 3, 2)).reshape(2, N_GRP, WIN_DEV, VS, F)
                crossed = cross_reference(sources, receivers)
                lagged = jnp.dot(transform, crossed, preferred_element_type=jnp.float32).astype(jnp.bfloat16)
                target_slot = slot_of_pair[source_block, column].astype(jnp.int32)
                return lax.dynamic_update_slice(buffer, lagged.reshape(1, LAGS, VS, CB), (target_slot, zero_index, zero_index, zero_index))
            return lax.cond(present, compute, lambda kept: kept, buffer)
        empty = jnp.zeros((PAIRS_MAX, LAGS, VS, CB), jnp.bfloat16)
        return lax.fori_loop(0, PAIRS_MAX, add_pair, empty)
    stacks = lax.map(column_stacks, jnp.arange(BLOCKS, dtype=jnp.int32))
    return jnp.transpose(stacks, (1, 2, 3, 0, 4)).reshape(PAIRS_MAX, LAGS, VS, BLOCKS * CB)
```

```python
import functools
import math

import jax
import jax.numpy as jnp
import ml_dtypes
import numpy as np
from jax import lax
from jax.experimental import pallas as pl
from jax.experimental.pallas import tpu as pltpu
from jax.sharding import PartitionSpec as P

F = 640
LAGS = 512
VS = 4
SLOTS = 8
WINDOWS = 128
NG = F // 8
ZS = 8
YS = 4
STAGES = ((0,), (1,), (2, 3))
MESH = pl.DeviceIdType.MESH
OFFSETS = ((1, 0), (0, 1), (1, 2), (0, 3), (1, 1), (0, 2), (1, 3))


def lag_rows():
    bins = np.arange(F)
    shifts = np.arange(LAGS) - LAGS // 2
    angles = math.pi / F * (shifts[:, None] * bins[None, :] % (2 * F))
    factor = 1.0 / math.sqrt(2.0 * WINDOWS * F)
    cos = (np.cos(angles) * factor).reshape(LAGS, NG, 1, 8)
    sin = (-np.sin(angles) * factor).reshape(LAGS, NG, 1, 8)
    return np.concatenate([cos, sin], axis=2).reshape(LAGS, 2 * F).astype(ml_dtypes.bfloat16)


def group_receivers(spec, rb, first, count):
    def step(n, carry):
        q = first + n
        x = spec[:, :, pl.ds(pl.multiple_of(q * 16, 16), 16), :].astype(jnp.float32)
        rb[2 * q] = x[:, :, :8, :].reshape(256, 128).astype(jnp.bfloat16)
        rb[2 * q + 1] = x[:, :, 8:, :].reshape(256, 128).astype(jnp.bfloat16)
        return carry

    lax.fori_loop(0, count, step, 0, unroll=2)


def own_sources(spec, turned, store):
    lane = lax.broadcasted_iota(jnp.int32, (256, 128), 1)
    for part in range(3):
        count = 32 if part < 2 else 16

        def step(q, acc, part=part):
            at = pl.multiple_of(part * 256 + q * 16, 16)
            x = spec[:, :, pl.ds(at, 16), :].astype(jnp.float32)
            low = jnp.where(lane < VS, x[:, :, :8, :].reshape(256, 128), 0.0)
            high = jnp.where(lane < VS, x[:, :, 8:, :].reshape(256, 128), 0.0)
            return acc + pltpu.roll(low, q * 8, 1) + pltpu.roll(high, q * 8 + 4, 1)

        acc = lax.fori_loop(0, count // 2, step, jnp.zeros((256, 128), jnp.float32), unroll=2)
        rows = acc.T
        for p in range(2):
            turned[p, part * 128 : part * 128 + count * VS, :] = rows[: count * VS, p * 128 : (p + 1) * 128]
    for s in range(VS):
        for p in range(2):
            store(s, p, turned[p, pl.ds(s, NG, stride=VS), :].astype(jnp.bfloat16))


def cross(rb, wide, crossed, count, first, groups):
    row = lax.broadcasted_iota(jnp.int32, (8, 128), 0)
    lane = lax.broadcasted_iota(jnp.int32, (8, 128), 1)
    mask = (lane % 8 == row).astype(jnp.float32)

    def step(n, carry):
        g = first + n
        left, right = [], []
        for si in range(count):
            for k in range(SLOTS):
                re = wide[si, 0, k, pl.ds(g, 1), :] * mask
                im = wide[si, 1, k, pl.ds(g, 1), :] * mask
                left.append(jnp.concatenate([re, im], 0).astype(jnp.bfloat16))
                right.append(jnp.concatenate([im, -re], 0).astype(jnp.bfloat16))
        rows = jnp.concatenate([jnp.concatenate(left, 0), jnp.concatenate(right, 0)], 1)
        got = jnp.dot(rows, rb[g], preferred_element_type=jnp.float32).astype(jnp.bfloat16)
        at = pl.multiple_of(g * 16, 16)
        for si in range(count):
            part = got[si * 128 : (si + 1) * 128].reshape(SLOTS, 16, 128)
            crossed[:, pl.ds(at, 16), si * 128 : (si + 1) * 128] = part
        return carry

    lax.fori_loop(0, groups, step, 0, unroll=min(groups, 8))


class Gather:
    def __init__(self, stage, buf, recv, send, place):
        self.stage, self.buf, self.recv, self.send = stage, buf, recv, send
        self.xl, self.z, self.c, self.grp = place

    def block(self, x_flip, dz):
        x = 1 - self.xl if x_flip else self.xl
        return (self.c * 2 + x) * ZS + lax.rem(self.z + dz + ZS, ZS)

    def device(self, xl, z, c):
        return (xl * (2 * ZS) + z * 2 + c, self.grp)

    def copy(self, block, to, recv, send):
        ref = self.buf.at[block]
        xl, z, c = self.xl, self.z, self.c
        if to == "x":
            xl = 1 - xl
        elif to == "core":
            c = 1 - c
        elif to == "up":
            z = lax.rem(z + 1, ZS)
        elif to == "down":
            z = lax.rem(z + ZS - 1, ZS)
        return pltpu.make_async_remote_copy(
            src_ref=ref,
            dst_ref=ref,
            send_sem=self.send.at[self.stage, send],
            recv_sem=self.recv.at[self.stage, recv],
            device_id=self.device(xl, z, c),
            device_id_type=MESH,
        )

    def ring(self, x_flip, up, h):
        return {(0, 1): 0, (0, 0): 4, (1, 1): 7, (1, 0): 10}[(x_flip, up)] + h

    def reach(self, x_flip, up):
        return 4 if x_flip != up else 3

    def forward(self, x_flip, up, h):
        if h < self.reach(x_flip, up):
            block = self.block(x_flip, -h if up else h)
            self.copy(block, "up" if up else "down", self.ring(x_flip, up, h + 1), 2).start()

    def start(self):
        own = self.block(0, 0)
        self.copy(own, "x", 0, 0).start()
        self.forward(0, 1, 0)
        self.forward(0, 0, 0)
        self.copy(own, "core", 15, 1).start()

    def partner(self):
        block = self.block(1, 0)
        self.copy(block, "x", 0, 0).wait_recv()
        self.forward(1, 1, 0)
        self.forward(1, 0, 0)
        self.copy(block, "core", 15, 1).start()

    def hop(self, h):
        for x_flip in (0, 1):
            for up in (1, 0):
                if h <= self.reach(x_flip, up):
                    block = self.block(x_flip, -h if up else h)
                    self.copy(block, "x", self.ring(x_flip, up, h), 0).wait_recv()
                    self.forward(x_flip, up, h)
                    self.copy(block, "core", 15, 1).start()

    def finish(self):
        half = pl.ds((1 - self.c) * (2 * ZS), 2 * ZS)
        self.copy(half, "core", 15, 1).wait_recv()

    def steps(self):
        return [self.start, self.partner] + [functools.partial(self.hop, h) for h in (1, 2, 3, 4)] + [self.finish]

    def drain(self):
        self.copy(self.block(0, 0), "x", 0, 0).wait_send()
        self.copy(pl.ds(0, 2 * ZS), "core", 15, 1).wait_send()
        self.copy(pl.ds(0, 14), "up", 1, 2).wait_send()


def kernel(spec, table, pattern, slots, out, rb, turned, wide, crossed, parts, arrived, g_recv, g_send, r_recv, r_send, *bufs):
    blk, grp = lax.axis_index("blk"), lax.axis_index("grp")
    xl, z, c = blk // (2 * ZS), lax.rem(blk // 2, ZS), lax.rem(blk, 2)
    xh, y = grp // YS, lax.rem(grp, YS)
    gathers = [Gather(n, bufs[n], g_recv, g_send, (xl, z, c, grp)) for n in range(len(STAGES))]

    def peer(flip, dy):
        side = 1 - xh if flip else xh
        return side * YS + lax.rem(y + dy + YS, YS)

    barrier = pltpu.get_barrier_semaphore()
    near = [
        gathers[0].device(1 - xl, z, c),
        gathers[0].device(xl, z, 1 - c),
        gathers[0].device(xl, lax.rem(z + 1, ZS), c),
        gathers[0].device(xl, lax.rem(z + ZS - 1, ZS), c),
    ] + [(blk, peer(*offset)) for offset in OFFSETS]
    for device in near:
        pl.semaphore_signal(barrier, inc=1, device_id=device, device_id_type=MESH)

    own = gathers[0].block(0, 0)

    def store(s, p, rows):
        for n, stage in enumerate(STAGES):
            if s in stage:
                bufs[n][own, stage.index(s), :, p * 128 : (p + 1) * 128] = rows

    own_sources(spec, turned, store)
    pl.semaphore_wait(barrier, len(near))

    pump = iter([step for gather in gathers for step in gather.steps()])
    done = [0]

    def pump_to(count):
        while done[0] < count:
            next(pump)()
            done[0] += 1

    per = len(gathers[0].steps())
    pump_to(1)

    def look(i, found):
        on = pattern[i, blk] > 0
        at = (lax.rem(i, 2) * 2 + i // (2 * ZS)) * ZS + lax.rem(i // 2, ZS)
        slot = slots[i, blk]
        return tuple(jnp.where(on & (slot == k), at, found[k]) for k in range(SLOTS))

    found = lax.fori_loop(0, 4 * ZS, look, (jnp.int32(-1),) * SLOTS)
    for n in range(5):
        group_receivers(spec, rb, n * 8, 8)
        pump_to(2 + n)
    pump_to(per)

    for n, stage in enumerate(STAGES):
        count = len(stage)
        last = n + 1 == len(STAGES)
        begin = per * (n + 1)

        def reach(part, last=last, begin=begin):
            if not last:
                pump_to(begin + part)

        reach(1)
        for si in range(count):
            for k in range(SLOTS):
                present = jnp.where(found[k] >= 0, 1.0, 0.0)
                rows = bufs[n][jnp.maximum(found[k], 0), si].astype(jnp.float32) * present
                for p in range(2):
                    wide[si, p, k] = rows[:, p * 128 : (p + 1) * 128]
        for piece in range(5):
            cross(rb, wide, crossed, count, piece * 16, 16)
            if piece % 2 == 1:
                reach(2 + piece // 2)
        lanes = 128 * count
        for m, offset in enumerate(OFFSETS + ((0, 0),)):
            k = peer(*offset)
            got = jnp.dot(table[...], crossed[k, :, :lanes], preferred_element_type=jnp.float32)
            got = got.astype(jnp.bfloat16)
            target = parts if m < len(OFFSETS) else arrived
            for si, s in enumerate(stage):
                target[k, s] = got[:, si * 128 : (si + 1) * 128]
            if m < len(OFFSETS):
                send_part(parts, arrived, r_send, r_recv, n, m, k, grp, (blk, k)).start()
            if m in (1, 3, 5):
                reach(4 + m // 2)
        reach(per)

    for n, stage in enumerate(STAGES):
        for m, (flip, dy) in enumerate(OFFSETS):
            source = peer(flip, -dy)
            send_part(parts, arrived, r_send, r_recv, n, m, source, source, (blk, source)).wait_recv()
        for s in stage:
            total = arrived[0, s].astype(jnp.float32)
            for g in range(1, SLOTS):
                total += arrived[g, s].astype(jnp.float32)
            out[s] = total.astype(jnp.bfloat16)
    for n in range(len(STAGES)):
        gathers[n].drain()
        for m, offset in enumerate(OFFSETS):
            k = peer(*offset)
            send_part(parts, arrived, r_send, r_recv, n, m, k, grp, (blk, k)).wait_send()


def send_part(parts, arrived, send, recv, n, m, k, row, device):
    stage = pl.ds(STAGES[n][0], len(STAGES[n]))
    return pltpu.make_async_remote_copy(
        src_ref=parts.at[k, stage],
        dst_ref=arrived.at[row, stage],
        send_sem=send.at[n, m],
        recv_sem=recv.at[n, m],
        device_id=device,
        device_id_type=MESH,
    )


def per_device(spectra, pattern, slot_of_pair, table):
    most = max(len(stage) for stage in STAGES)
    vmem = pl.BlockSpec(memory_space=pltpu.VMEM)
    smem = pl.BlockSpec(memory_space=pltpu.SMEM)
    stacks = pl.pallas_call(
        kernel,
        out_shape=jax.ShapeDtypeStruct((VS, LAGS, 128), jnp.bfloat16),
        in_specs=[vmem, vmem, smem, smem],
        out_specs=vmem,
        scratch_shapes=[
            pltpu.VMEM((NG, 256, 128), jnp.bfloat16),
            pltpu.VMEM((2, 3 * 128, 128), jnp.float32),
            pltpu.VMEM((most, 2, SLOTS, NG, 128), jnp.float32),
            pltpu.VMEM((SLOTS, 2 * F, 128 * most), jnp.bfloat16),
            pltpu.VMEM((SLOTS, VS, LAGS, 128), jnp.bfloat16),
            pltpu.VMEM((SLOTS, VS, LAGS, 128), jnp.bfloat16),
            pltpu.SemaphoreType.DMA((len(STAGES), 16)),
            pltpu.SemaphoreType.DMA((len(STAGES), 3)),
            pltpu.SemaphoreType.DMA((len(STAGES), len(OFFSETS))),
            pltpu.SemaphoreType.DMA((len(STAGES), len(OFFSETS))),
        ]
        + [pltpu.VMEM((4 * ZS, len(stage), NG, 256), jnp.bfloat16) for stage in STAGES],
        compiler_params=pltpu.CompilerParams(collective_id=0, has_side_effects=True, vmem_limit_bytes=56 << 20),
        name="correlate",
    )(spectra, table, pattern, slot_of_pair)
    return jnp.transpose(stacks, (1, 0, 2))[None]


def solution(mesh):
    mapped = jax.shard_map(
        per_device,
        mesh=mesh,
        in_specs=(P(None, "grp", None, "blk"), P(), P(), P()),
        out_specs=P("grp", None, None, "blk"),
        check_vma=False,
    )
    return lambda spectra, pattern, slot_of_pair: mapped(spectra, pattern, slot_of_pair, jnp.asarray(lag_rows()))
```

```python
import functools
import math

import jax
import jax.numpy as jnp
import ml_dtypes
import numpy as np
from jax import lax
from jax.experimental import pallas as pl
from jax.experimental.pallas import tpu as pltpu
from jax.sharding import PartitionSpec as P

F = 640
LAGS = 512
VS = 4
SLOTS = 8
WINDOWS = 128
NG = F // 8
ZS = 8
YS = 4
NQ = NG // 2
MESH = pl.DeviceIdType.MESH
FIRST = 256
REST = LAGS - FIRST


def lag_rows():
    bins = np.arange(F)
    shifts = np.arange(LAGS) - LAGS // 2
    angles = math.pi / F * (shifts[:, None] * bins[None, :] % (2 * F))
    factor = 1.0 / math.sqrt(2.0 * WINDOWS * F)
    both = np.stack([np.cos(angles), -np.sin(angles)], axis=1) * factor
    both = both.reshape(LAGS, 2, NQ, 2, 8).transpose(0, 3, 2, 1, 4)
    return both.reshape(LAGS, 2 * F).astype(ml_dtypes.bfloat16)


def group_receivers(spec, rb, first, count):
    def step(n, carry):
        q = first + n
        x = spec[:, :, pl.ds(pl.multiple_of(q * 16, 16), 16), :].astype(jnp.float32)
        rb[q] = x[:, :, :8, :].reshape(256, 128).astype(jnp.bfloat16)
        rb[NQ + q] = x[:, :, 8:, :].reshape(256, 128).astype(jnp.bfloat16)
        return carry

    lax.fori_loop(0, count, step, 0, unroll=2)


def own_sources(spec, turned, loaded, store):
    lane = lax.broadcasted_iota(jnp.int32, (8, 128), 1)
    for begin, count in ((0, 32), (32, NQ - 32)):

        def step(q, acc, begin=begin):
            x = spec[:, :, pl.ds(pl.multiple_of((begin + q) * 16, 16), 16), :].astype(jnp.float32)
            x = jnp.where(lane < VS, x.reshape(32, 2, 8, 128), 0.0).reshape(512, 128)
            return acc + pltpu.roll(x, q * VS, 1)

        acc = jnp.zeros((512, 128), jnp.float32)
        for chunk in range(count // 8):
            loaded(begin // 8 + chunk)
            acc = lax.fori_loop(chunk * 8, chunk * 8 + 8, step, acc, unroll=8)
        acc = acc.reshape(32, 2, 8, 128)
        for h in range(2):
            rows = acc[:, h].reshape(256, 128).T
            for p in range(2):
                turned[h, p, begin * VS : (begin + count) * VS, :] = rows[: count * VS, p * 128 : (p + 1) * 128]
    for s in range(VS):
        for h in range(2):
            for p in range(2):
                store(s, h, p, turned[h, p, pl.ds(s, NQ, stride=VS), :].astype(jnp.bfloat16))


def cross(rb, wide, crossed, count, first, groups):
    row = lax.broadcasted_iota(jnp.int32, (8, 128), 0)
    lane = lax.broadcasted_iota(jnp.int32, (8, 128), 1)
    mask = (lane % 8 == row).astype(jnp.float32)

    def step(n, carry):
        g = first + n
        left, right = [], []
        for si in range(count):
            for k in range(SLOTS):
                re = wide[si, 0, k, pl.ds(g, 1), :] * mask
                im = wide[si, 1, k, pl.ds(g, 1), :] * mask
                left.append(jnp.concatenate([re, im], 0).astype(jnp.bfloat16))
                right.append(jnp.concatenate([im, -re], 0).astype(jnp.bfloat16))
        rows = jnp.concatenate([jnp.concatenate(left, 0), jnp.concatenate(right, 0)], 1)
        got = jnp.dot(rows, rb[g], preferred_element_type=jnp.float32).astype(jnp.bfloat16)
        at = pl.multiple_of(g * 16, 16)
        for si in range(count):
            part = got[si * 128 : (si + 1) * 128].reshape(SLOTS, 16, 128)
            crossed[:, pl.ds(at, 16), si * 128 : (si + 1) * 128] = part
        return carry

    lax.fori_loop(0, groups, step, 0, unroll=16)


class Place:
    def __init__(self):
        blk, grp = lax.axis_index("blk"), lax.axis_index("grp")
        self.blk, self.grp = blk, grp
        self.xl, self.z, self.c = blk // (2 * ZS), lax.rem(blk // 2, ZS), lax.rem(blk, 2)
        self.xh, self.y = grp // YS, lax.rem(grp, YS)

    def near(self, flip_x=False, dz=0, flip_core=False):
        xl = 1 - self.xl if flip_x else self.xl
        c = 1 - self.c if flip_core else self.c
        return (xl * (2 * ZS) + lax.rem(self.z + dz + ZS, ZS) * 2 + c, self.grp)

    def far(self, flip_x=False, dy=0):
        xh = 1 - self.xh if flip_x else self.xh
        return (self.blk, xh * YS + lax.rem(self.y + dy, YS))


OWN = 2
X_SEND, CORE_SEND, Z_SEND = 0, 1, 2
CORE_RECV = 15


def at_z(dz):
    return (dz + OWN) % ZS


class Gather:
    def __init__(self, n, buf, recv, send, place):
        self.buf, self.recv, self.send, self.place = buf, recv.at[n], send.at[n], place

    def copy(self, src, dst, to, recv, send):
        return pltpu.make_async_remote_copy(
            src_ref=self.buf.at[pl.ds(*src)],
            dst_ref=self.buf.at[pl.ds(*dst)],
            send_sem=self.send.at[send],
            recv_sem=self.recv.at[recv],
            device_id=to,
            device_id_type=MESH,
        )

    def wait(self, blocks, recv):
        self.copy(blocks, blocks, self.place.near(True), recv, X_SEND).wait_recv()

    def to_core(self, first, count):
        self.copy((first, count), (2 * ZS + first, count), self.place.near(flip_core=True), CORE_RECV, CORE_SEND).start()

    def finish(self):
        self.wait((2 * ZS, 2 * ZS), CORE_RECV)

    def drain(self):
        for count, send in ((self.X_BLOCKS, X_SEND), (2 * ZS, CORE_SEND), (self.Z_BLOCKS, Z_SEND)):
            self.copy((0, count), (0, count), self.place.near(True), 0, send).wait_send()


class Ring(Gather):
    X_BLOCKS, Z_BLOCKS = 1, 14

    @staticmethod
    def index(flip_x, dz, flip_core):
        return (flip_core * ZS + lax.rem(dz + OWN, ZS)) * 2 + flip_x

    def start(self):
        self.copy((2 * OWN, 1), (2 * OWN + 1, 1), self.place.near(True), 0, X_SEND).start()

    def partner(self):
        self.wait((2 * OWN + 1, 1), 0)
        for sign, first in ((1, 1), (-1, 5)):
            self.copy((2 * OWN, 2), (2 * at_z(-sign), 2), self.place.near(dz=sign), first, Z_SEND).start()
        self.to_core(2 * OWN, 2)

    def hop(self, h):
        for sign, first in ((1, 0), (-1, 4)):
            single = 0 if sign > 0 else 1
            here, there = 2 * at_z(-h * sign), 2 * at_z(-(h + 1) * sign)
            blocks = (here, 2) if h < 4 else (here + single, 1)
            self.wait(blocks, first + h)
            ahead = self.place.near(dz=sign)
            if h < 3:
                self.copy(blocks, (there, 2), ahead, first + h + 1, Z_SEND).start()
            elif h == 3:
                self.copy((here + single, 1), (there + single, 1), ahead, first + 4, Z_SEND).start()
            self.to_core(*blocks)

    def steps(self):
        return [self.start, self.partner] + [functools.partial(self.hop, h) for h in (1, 2, 3, 4)] + [self.finish]


class Direct(Gather):
    X_BLOCKS, Z_BLOCKS = 8, 7
    NEAR, FAR = (0, 5), (5, 3)

    @staticmethod
    def index(flip_x, dz, flip_core):
        return (flip_core * 2 + flip_x) * ZS + lax.rem(dz + OWN, ZS)

    def start(self):
        for dz in (1, -1, 2, -2):
            self.copy((OWN, 1), (at_z(-dz), 1), self.place.near(dz=dz), 0, Z_SEND).start()

    def onward(self, blocks, recv):
        first, count = blocks
        self.copy(blocks, (ZS + first, count), self.place.near(True), recv, X_SEND).start()
        self.to_core(*blocks)

    def second(self):
        place = self.place
        self.wait((0, 4), 0)
        for sign in (1, -1):
            self.copy((at_z(-2 * sign), 1), (at_z(-3 * sign), 1), place.near(dz=sign), 1, Z_SEND).start()
        sign = 1 - 2 * place.c
        self.copy((OWN - 2 * sign, 1), (at_z(4), 1), place.near(dz=2 * sign), 1, Z_SEND).start()
        self.onward(self.NEAR, 2)

    def third(self):
        self.wait(self.FAR, 1)
        self.onward(self.FAR, 3)

    def from_x(self, blocks, recv):
        first, count = blocks
        self.wait((ZS + first, count), recv)
        self.to_core(ZS + first, count)

    def steps(self):
        return [
            self.start,
            self.second,
            self.third,
            lambda: self.from_x(self.NEAR, 2),
            lambda: self.from_x(self.FAR, 3),
            self.finish,
        ]


class Reduce:
    def __init__(self, s, place, bufs, send, recv):
        self.s, self.place = s, place
        self.parts, self.over_x, self.after_x, self.over_y, self.side, self.after_y = (buf.at[s] for buf in bufs)
        self.send, self.recv = send.at[s], recv.at[s]

    def copy(self, src, dst, sem, to):
        return pltpu.make_async_remote_copy(
            src_ref=src,
            dst_ref=dst,
            send_sem=self.send.at[sem],
            recv_sem=self.recv.at[sem],
            device_id=to,
            device_id_type=MESH,
        )

    def sent_slot(self, dy):
        place = self.place
        at = lax.rem(place.y + dy, YS)
        src = self.parts.at[1 - place.xh, at, pl.ds(0, FIRST)]
        self.copy(src, self.over_x.at[at], 0, place.far(True)).start()

    def sent_row(self, dy):
        at = lax.rem(self.place.y + dy, YS)
        src = self.parts.at[:, at, pl.ds(FIRST, REST)]
        self.copy(src, self.over_y.at[dy - 1], 1, self.place.far(dy=dy)).start()

    def wait(self, ref, sem):
        self.copy(ref, ref, sem, self.place.far(True)).wait_recv()

    def combine_x(self):
        place = self.place
        self.wait(self.over_x, 0)
        for dy in (2, 1, 3):
            at = lax.rem(place.y + dy, YS)
            own = self.parts[place.xh, at, :FIRST].astype(jnp.float32)
            self.over_x[at] = (own + self.over_x[at].astype(jnp.float32)).astype(jnp.bfloat16)
            self.copy(self.over_x.at[at], self.after_x.at[dy - 1], 2, place.far(dy=dy)).start()

    def along_y(self, xh):
        total = self.parts[xh, self.place.y, FIRST:].astype(jnp.float32)
        for m in range(YS - 1):
            total += self.over_y[m, xh].astype(jnp.float32)
        return total

    def combine_y(self):
        self.wait(self.over_y, 1)
        self.side[...] = self.along_y(1 - self.place.xh).astype(jnp.bfloat16)
        self.copy(self.side, self.after_y, 3, self.place.far(True)).start()

    def final(self, out):
        place, s = self.place, self.s
        self.wait(self.after_x, 2)
        total = self.parts[place.xh, place.y, :FIRST].astype(jnp.float32)
        total += self.over_x[place.y].astype(jnp.float32)
        for m in range(YS - 1):
            total += self.after_x[m].astype(jnp.float32)
        out[pl.ds(s, FIRST, stride=VS), :] = total
        rest = self.along_y(place.xh)
        self.wait(self.after_y, 3)
        out[pl.ds(FIRST * VS + s, REST, stride=VS), :] = rest + self.after_y[...].astype(jnp.float32)

    def drain(self):
        for ref, sem in ((self.over_x, 0), (self.over_y, 1), (self.after_x, 2), (self.after_y, 3)):
            self.copy(ref, ref, sem, self.place.far(True)).wait_send()


STAGES = ((0,), (1,), (2, 3))
KINDS = (Direct, Ring, Ring)
MOST = max(len(stage) for stage in STAGES)
PROGRAM = (
    ("gather", 0),
    ("gather", 1),
    ("gather", 2),
    ("group", 0),
    ("group", 1),
    ("group", 2),
    ("group", 3),
    ("group", 4),
    ("gather", 1),
    ("gather", 2),
    ("gather", 0),
    ("gather", 1),
    ("gather", 0),
    ("gather", 0),
    ("gather", 2),
    ("gather", 1),
    ("gather", 0),
    ("gather", 0),
    ("select", 0),
    ("cross", 0, 0),
    ("cross", 0, 1),
    ("cross", 0, 2),
    ("cross", 0, 3),
    ("cross", 0, 4),
    ("lags", 0, 0),
    ("gather", 1),
    ("gather", 2),
    ("lags", 0, 1),
    ("lags", 0, 2),
    ("lags", 0, 3),
    ("gather", 1),
    ("gather", 1),
    ("select", 1),
    ("cross", 1, 0),
    ("cross", 1, 1),
    ("cross", 1, 2),
    ("gather", 2),
    ("cross", 1, 3),
    ("after_y", 0),
    ("cross", 1, 4),
    ("lags", 1, 0),
    ("after_x", 0),
    ("lags", 1, 1),
    ("gather", 2),
    ("lags", 1, 2),
    ("lags", 1, 3),
    ("gather", 2),
    ("select", 2),
    ("cross", 2, 0),
    ("cross", 2, 1),
    ("cross", 2, 2),
    ("cross", 2, 3),
    ("cross", 2, 4),
    ("lags", 2, 0),
    ("after_x", 1),
    ("lags", 2, 1),
    ("after_y", 1),
    ("lags", 2, 2),
    ("lags", 2, 3),
    ("final", 0),
    ("final", 1),
    ("after_x", 2),
    ("after_x", 3),
    ("after_y", 2),
    ("after_y", 3),
    ("final", 2),
    ("final", 3),
)


def kernel(spectra, lag_table, pattern, slots, out, rb, turned, wide, crossed, spec, table, load, *rest):
    sums, (g_send, g_recv, r_send, r_recv), bufs = rest[:6], rest[6:10], rest[10:]
    loads = []
    for n in range(5):
        bins = pl.ds(n * 128, 128)
        loads.append(pltpu.make_async_copy(spectra.at[:, :, bins], spec.at[:, :, bins], load.at[n]))
    loads.append(pltpu.make_async_copy(lag_table, table, load.at[5]))
    for copy in loads:
        copy.start()
    place = Place()
    blk = place.blk
    barrier = pltpu.get_barrier_semaphore()
    peers = [place.near(True), place.near(flip_core=True)] + [place.near(dz=dz) for dz in (1, -1, 2, -2)]
    peers += [place.far(True)] + [place.far(dy=dy) for dy in (1, 2, 3)]
    for device in peers:
        pl.semaphore_signal(barrier, inc=1, device_id=device, device_id_type=MESH)

    def store(s, h, p, rows):
        for n, stage in enumerate(STAGES):
            if s in stage:
                own = 2 * OWN if KINDS[n] is Ring else OWN
                bufs[n][own, stage.index(s), h * NQ : (h + 1) * NQ, p * 128 : (p + 1) * 128] = rows

    own_sources(spec, turned, lambda n: loads[n].wait(), store)
    pl.semaphore_wait(barrier, len(peers))

    gathers = [KINDS[n](n, bufs[n], g_recv, g_send, place) for n in range(len(STAGES))]
    reduces = [Reduce(s, place, sums, r_send, r_recv) for s in range(VS)]
    steps = [iter(gather.steps()) for gather in gathers]

    def look(i, found):
        on = pattern[i, blk] > 0
        flip_x = jnp.abs(i // (2 * ZS) - place.xl)
        flip_core = jnp.abs(lax.rem(i, 2) - place.c)
        dz = lax.rem(lax.rem(i // 2, ZS) - place.z + ZS, ZS)
        slot = slots[i, blk]
        rule = [kind.index(flip_x, dz, flip_core) for kind in (Direct, Ring)]
        return tuple(
            tuple(jnp.where(on & (slot == k), at, old[k]) for k in range(SLOTS)) for at, old in zip(rule, found)
        )

    found = lax.fori_loop(0, 4 * ZS, look, ((jnp.int32(-1),) * SLOTS,) * 2)

    loads[5].wait()

    def select(n):
        block = found[0 if KINDS[n] is Direct else 1]
        for k in range(SLOTS):
            present = jnp.where(block[k] >= 0, 1.0, 0.0)
            for si in range(len(STAGES[n])):
                rows = bufs[n][jnp.maximum(block[k], 0), si].astype(jnp.float32) * present
                for p in range(2):
                    wide[si, p, k] = rows[:, p * 128 : (p + 1) * 128]

    def lags(n, number):
        stage, dy = STAGES[n], (2, 1, 3, 0)[number]
        at = lax.rem(place.y + dy, YS)
        for other in (True, False):
            xh = 1 - place.xh if other else place.xh
            rows = crossed[xh * YS + at, :, : 128 * len(stage)]
            got = jnp.dot(table[...], rows, preferred_element_type=jnp.float32).astype(jnp.bfloat16)
            for si, s in enumerate(stage):
                sums[0][s, xh, at] = got[:, si * 128 : (si + 1) * 128]
                if other:
                    reduces[s].sent_slot(dy)
        if dy:
            for s in stage:
                reduces[s].sent_row(dy)

    run = {
        "gather": lambda n: next(steps[n])(),
        "group": lambda n: group_receivers(spec, rb, n * 8, 8),
        "select": select,
        "cross": lambda n, piece: cross(rb, wide, crossed, len(STAGES[n]), piece * 16, 16),
        "lags": lags,
        "after_x": lambda s: reduces[s].combine_x(),
        "after_y": lambda s: reduces[s].combine_y(),
        "final": lambda s: reduces[s].final(out),
    }
    for name, *arguments in PROGRAM:
        run[name](*arguments)
    for gather in gathers:
        gather.drain()
    for s in range(VS):
        reduces[s].drain()


def per_device(spectra, pattern, slot_of_pair, table):
    vmem = pl.BlockSpec(memory_space=pltpu.VMEM)
    smem = pl.BlockSpec(memory_space=pltpu.SMEM)
    hbm = pl.BlockSpec(memory_space=pl.ANY)
    stacks = pl.pallas_call(
        kernel,
        out_shape=jax.ShapeDtypeStruct((LAGS * VS, 128), jnp.float32),
        in_specs=[hbm, hbm, smem, smem],
        out_specs=vmem,
        scratch_shapes=[
            pltpu.VMEM((NG, 256, 128), jnp.bfloat16),
            pltpu.VMEM((2, 2, 2 * 128, 128), jnp.float32),
            pltpu.VMEM((MOST, 2, SLOTS, NG, 128), jnp.float32),
            pltpu.VMEM((SLOTS, 2 * F, 128 * MOST), jnp.bfloat16),
            pltpu.VMEM((2, WINDOWS // 8, F, 128), jnp.bfloat16),
            pltpu.VMEM((LAGS, 2 * F), jnp.bfloat16),
            pltpu.SemaphoreType.DMA((6,)),
            pltpu.VMEM((VS, 2, YS, LAGS, 128), jnp.bfloat16),
            pltpu.VMEM((VS, YS, FIRST, 128), jnp.bfloat16),
            pltpu.VMEM((VS, YS - 1, FIRST, 128), jnp.bfloat16),
            pltpu.VMEM((VS, YS - 1, 2, REST, 128), jnp.bfloat16),
            pltpu.VMEM((VS, REST, 128), jnp.bfloat16),
            pltpu.VMEM((VS, REST, 128), jnp.bfloat16),
            pltpu.SemaphoreType.DMA((len(STAGES), 3)),
            pltpu.SemaphoreType.DMA((len(STAGES), 16)),
            pltpu.SemaphoreType.DMA((VS, 4)),
            pltpu.SemaphoreType.DMA((VS, 4)),
                ]
        + [pltpu.VMEM((4 * ZS, len(stage), NG, 256), jnp.bfloat16) for stage in STAGES],
        compiler_params=pltpu.CompilerParams(collective_id=0, has_side_effects=True, vmem_limit_bytes=56 << 20),
        name="correlate",
    )(spectra, table, pattern, slot_of_pair)
    return stacks.astype(jnp.bfloat16).reshape(1, LAGS, VS, 128)


def solution(mesh):
    mapped = jax.shard_map(
        per_device,
        mesh=mesh,
        in_specs=(P(None, "grp", None, "blk"), P(), P(), P()),
        out_specs=P("grp", None, None, "blk"),
        check_vma=False,
    )
    return lambda spectra, pattern, slot_of_pair: mapped(spectra, pattern, slot_of_pair, jnp.asarray(lag_rows()))
```

```python
import functools
import math

import jax
import jax.numpy as jnp
import ml_dtypes
import numpy as np
from jax import lax
from jax.experimental import pallas as pl
from jax.experimental.pallas import tpu as pltpu
from jax.sharding import PartitionSpec as P

F = 640
LAGS = 512
VS = 4
SLOTS = 8
WINDOWS = 128
NG = F // 8
ZS = 8
YS = 4
NQ = NG // 2
MESH = pl.DeviceIdType.MESH
FIRST = 256
REST = LAGS - FIRST
HALF = REST // 2


def lag_rows():
    bins = np.arange(F)
    shifts = np.arange(LAGS) - LAGS // 2
    angles = math.pi / F * (shifts[:, None] * bins[None, :] % (2 * F))
    factor = 1.0 / math.sqrt(2.0 * WINDOWS * F)
    both = np.stack([np.cos(angles), -np.sin(angles)], axis=1) * factor
    both = both.reshape(LAGS, 2, NQ, 2, 8).transpose(0, 3, 2, 1, 4)
    return both.reshape(LAGS, 2 * F).astype(ml_dtypes.bfloat16)


def group_receivers(spec, rb, first, count):
    def step(n, carry):
        q = first + n
        x = spec[:, :, pl.ds(pl.multiple_of(q * 16, 16), 16), :].astype(jnp.float32)
        rb[q] = x[:, :, :8, :].reshape(256, 128).astype(jnp.bfloat16)
        rb[NQ + q] = x[:, :, 8:, :].reshape(256, 128).astype(jnp.bfloat16)
        return carry

    lax.fori_loop(0, count, step, 0, unroll=2)


def own_sources(spec, turned, loaded, store):
    lane = lax.broadcasted_iota(jnp.int32, (8, 128), 1)
    for begin, count in ((0, 32), (32, NQ - 32)):

        def step(q, acc, begin=begin):
            x = spec[:, :, pl.ds(pl.multiple_of((begin + q) * 16, 16), 16), :].astype(jnp.float32)
            x = jnp.where(lane < VS, x.reshape(32, 2, 8, 128), 0.0).reshape(512, 128)
            return acc + pltpu.roll(x, q * VS, 1)

        acc = jnp.zeros((512, 128), jnp.float32)
        for chunk in range(count // 8):
            loaded(begin // 8 + chunk)
            acc = lax.fori_loop(chunk * 8, chunk * 8 + 8, step, acc, unroll=8)
        acc = acc.reshape(32, 2, 8, 128)
        for h in range(2):
            rows = acc[:, h].reshape(256, 128).T
            for p in range(2):
                turned[h, p, begin * VS : (begin + count) * VS, :] = rows[: count * VS, p * 128 : (p + 1) * 128]
    for s in range(VS):
        for h in range(2):
            for p in range(2):
                store(s, h, p, turned[h, p, pl.ds(s, NQ, stride=VS), :].astype(jnp.bfloat16))


def cross(rb, wide, crossed, count, first, groups):
    row = lax.broadcasted_iota(jnp.int32, (8, 128), 0)
    lane = lax.broadcasted_iota(jnp.int32, (8, 128), 1)
    mask = (lane % 8 == row).astype(jnp.float32)

    def step(n, carry):
        g = first + n
        left, right = [], []
        for si in range(count):
            for k in range(SLOTS):
                re = wide[si, 0, k, pl.ds(g, 1), :] * mask
                im = wide[si, 1, k, pl.ds(g, 1), :] * mask
                left.append(jnp.concatenate([re, im], 0).astype(jnp.bfloat16))
                right.append(jnp.concatenate([im, -re], 0).astype(jnp.bfloat16))
        rows = jnp.concatenate([jnp.concatenate(left, 0), jnp.concatenate(right, 0)], 1)
        got = jnp.dot(rows, rb[g], preferred_element_type=jnp.float32).astype(jnp.bfloat16)
        at = pl.multiple_of(g * 16, 16)
        for si in range(count):
            part = got[si * 128 : (si + 1) * 128].reshape(SLOTS, 16, 128)
            crossed[:, pl.ds(at, 16), si * 128 : (si + 1) * 128] = part
        return carry

    lax.fori_loop(0, groups, step, 0, unroll=16)


class Place:
    def __init__(self):
        blk, grp = lax.axis_index("blk"), lax.axis_index("grp")
        self.blk, self.grp = blk, grp
        self.xl, self.z, self.c = blk // (2 * ZS), lax.rem(blk // 2, ZS), lax.rem(blk, 2)
        self.xh, self.y = grp // YS, lax.rem(grp, YS)
        self.known = {}

    def once(self, key, make):
        if key not in self.known:
            self.known[key] = make()
        return self.known[key]

    def near(self, flip_x=False, dz=0, flip_core=False):
        xl = 1 - self.xl if flip_x else self.xl
        c = 1 - self.c if flip_core else self.c
        at = lambda: xl * (2 * ZS) + lax.rem(self.z + dz + ZS, ZS) * 2 + c
        if not isinstance(dz, int):
            return (at(), self.grp)
        return (self.once(("near", flip_x, dz, flip_core), at), self.grp)

    def slot(self, flip_x, dy):
        xh = 1 - self.xh if flip_x else self.xh
        return self.once(("slot", flip_x, dy), lambda: xh * YS + lax.rem(self.y + dy, YS))

    def far(self, flip_x=False, dy=0):
        return (self.blk, self.slot(flip_x, dy))


OWN = 2
X_SEND, CORE_SEND, Z_SEND = 0, 1, 2
CORE_RECV = 15


def at_z(dz, own=OWN):
    return (dz + own) % ZS


class Gather:
    def __init__(self, n, buf, recv, send, place):
        self.buf, self.recv, self.send, self.place = buf, recv.at[n], send.at[n], place

    def copy(self, src, dst, to, recv, send):
        return pltpu.make_async_remote_copy(
            src_ref=self.buf.at[pl.ds(*src)],
            dst_ref=self.buf.at[pl.ds(*dst)],
            send_sem=self.send.at[send],
            recv_sem=self.recv.at[recv],
            device_id=to,
            device_id_type=MESH,
        )

    def wait(self, blocks, recv):
        self.copy(blocks, blocks, self.place.near(True), recv, X_SEND).wait_recv()

    def to_core(self, first, count):
        self.copy((first, count), (2 * ZS + first, count), self.place.near(flip_core=True), CORE_RECV, CORE_SEND).start()

    def finish(self):
        self.wait((2 * ZS, 2 * ZS), CORE_RECV)

    def drain(self):
        for count, send in ((self.X_BLOCKS, X_SEND), (2 * ZS, CORE_SEND), (self.Z_BLOCKS, Z_SEND)):
            self.copy((0, count), (0, count), self.place.near(True), 0, send).wait_send()


class Ring(Gather):
    X_BLOCKS, Z_BLOCKS, OWN = 1, 14, 1

    @staticmethod
    def index(flip_x, dz, flip_core):
        return (flip_core * ZS + lax.rem(dz + 1, ZS)) * 2 + flip_x

    def start(self):
        self.copy((2, 1), (3, 1), self.place.near(True), 0, X_SEND).start()

    def partner(self):
        self.wait((3, 1), 0)
        for sign, first in ((1, 1), (-1, 5)):
            self.copy((2, 2), (2 * at_z(-sign, 1), 2), self.place.near(dz=sign), first, Z_SEND).start()

    def hop(self, h):
        for sign, first in ((1, 0), (-1, 4)):
            single = 0 if sign > 0 else 1
            here, there = 2 * at_z(-h * sign, 1), 2 * at_z(-(h + 1) * sign, 1)
            blocks = (here, 2) if h < 4 else (here + single, 1)
            self.wait(blocks, first + h)
            ahead = self.place.near(dz=sign)
            if h < 3:
                self.copy(blocks, (there, 2), ahead, first + h + 1, Z_SEND).start()
            elif h == 3:
                self.copy((here + single, 1), (there + single, 1), ahead, first + 4, Z_SEND).start()
        for blocks in {1: ((0, 6),), 3: ((6, 4), (12, 4)), 4: ((10, 2),)}.get(h, ()):
            self.to_core(*blocks)

    def steps(self):
        return [self.start, self.partner] + [functools.partial(self.hop, h) for h in (1, 2, 3, 4)] + [self.finish]


class Direct(Gather):
    X_BLOCKS, Z_BLOCKS = 8, 7
    NEAR, FAR = (0, 5), (5, 3)

    @staticmethod
    def index(flip_x, dz, flip_core):
        return (flip_core * 2 + flip_x) * ZS + lax.rem(dz + OWN, ZS)

    def start(self):
        for dz in (1, -1, 2, -2):
            self.copy((OWN, 1), (at_z(-dz), 1), self.place.near(dz=dz), 0, Z_SEND).start()

    def onward(self, blocks, recv):
        first, count = blocks
        self.copy(blocks, (ZS + first, count), self.place.near(True), recv, X_SEND).start()
        self.to_core(*blocks)

    def second(self):
        place = self.place
        self.wait((0, 4), 0)
        for sign in (1, -1):
            self.copy((at_z(-2 * sign), 1), (at_z(-3 * sign), 1), place.near(dz=sign), 1, Z_SEND).start()
        sign = 1 - 2 * place.c
        self.copy((OWN - 2 * sign, 1), (at_z(4), 1), place.near(dz=2 * sign), 1, Z_SEND).start()
        self.onward(self.NEAR, 2)

    def third(self):
        self.wait(self.FAR, 1)
        self.onward(self.FAR, 3)

    def from_x(self, blocks, recv):
        first, count = blocks
        self.wait((ZS + first, count), recv)
        self.to_core(ZS + first, count)

    def steps(self):
        return [
            self.start,
            self.second,
            self.third,
            lambda: self.from_x(self.NEAR, 2),
            lambda: self.from_x(self.FAR, 3),
            self.finish,
        ]


STAGES = ((0,), (1, 2), (3,))
KINDS = (Direct, Ring, Ring)
MOST = max(len(stage) for stage in STAGES)
TURNS = (2, 1, 3, 0)


class Reduce:
    def __init__(self, n, place, bufs, send, recv):
        self.stage, self.place = STAGES[n], place
        part = pl.ds(STAGES[n][0], len(STAGES[n]))
        refs = (buf.at[part] for buf in bufs)
        self.parts, self.over_x, self.after_x, self.over_y, self.side, self.after_y, self.passing = refs
        self.send, self.recv = send.at[n], recv.at[n]

    def copy(self, src, dst, sem, to):
        return pltpu.make_async_remote_copy(
            src_ref=src,
            dst_ref=dst,
            send_sem=self.send.at[sem],
            recv_sem=self.recv.at[sem],
            device_id=to,
            device_id_type=MESH,
        )

    def sent(self, turn):
        if turn % 2:
            two = pl.ds(turn - 1, 2)
            src = self.parts.at[:, 1, two, pl.ds(0, FIRST)]
            self.copy(src, self.over_x.at[:, two], 0, self.place.far(True)).start()
        if turn == 0:
            for half, dy in ((0, 1), (1, 3)):
                src = self.parts.at[:, :, 0, pl.ds(FIRST + half * HALF, HALF)]
                self.copy(src, self.passing.at[:, :, half], 4, self.place.far(dy=dy)).start()
        elif turn < YS - 1:
            self.along(turn, turn % 2)

    def along(self, turn, half):
        rows = pl.ds(FIRST + half * HALF, HALF)
        to = self.place.far(dy=TURNS[turn])
        self.copy(self.parts.at[:, :, turn, rows], self.over_y.at[:, turn - 1, :, half], 1, to).start()

    def relay(self):
        self.wait(self.passing, 4)
        for half in range(2):
            begin = FIRST + half * HALF
            for si in range(len(self.stage)):
                for side in range(2):
                    own = self.parts[si, side, 1 + half, begin : begin + HALF].astype(jnp.float32)
                    own += self.passing[si, side, half].astype(jnp.float32)
                    self.parts[si, side, 1 + half, begin : begin + HALF] = own.astype(jnp.bfloat16)
            self.along(1 + half, half)

    def wait(self, ref, sem):
        self.copy(ref, ref, sem, self.place.far(True)).wait_recv()

    def combine_x(self):
        self.wait(self.over_x, 0)
        for turn in range(YS - 1):
            for si in range(len(self.stage)):
                own = self.parts[si, 0, turn, :FIRST].astype(jnp.float32)
                self.over_x[si, turn] = (own + self.over_x[si, turn].astype(jnp.float32)).astype(jnp.bfloat16)
            self.copy(self.over_x.at[:, turn], self.after_x.at[:, turn], 2, self.place.far(dy=TURNS[turn])).start()

    def along_y(self, si, side):
        total = self.parts[si, side, YS - 1, FIRST:].astype(jnp.float32)
        for m in range(2):
            total += self.over_y[si, m, side].astype(jnp.float32).reshape(REST, 128)
        return total

    def combine_y(self):
        self.wait(self.over_y, 1)
        for si in range(len(self.stage)):
            self.side[si] = self.along_y(si, 1).astype(jnp.bfloat16)
        self.copy(self.side, self.after_y, 3, self.place.far(True)).start()

    def final(self, out):
        self.wait(self.after_x, 2)
        self.wait(self.after_y, 3)
        for si, s in enumerate(self.stage):
            total = self.parts[si, 0, YS - 1, :FIRST].astype(jnp.float32)
            total += self.over_x[si, YS - 1].astype(jnp.float32)
            for turn in range(YS - 1):
                total += self.after_x[si, turn].astype(jnp.float32)
            out[pl.ds(s, FIRST, stride=VS), :] = total
            rest = self.along_y(si, 0) + self.after_y[si].astype(jnp.float32)
            out[pl.ds(FIRST * VS + s, REST, stride=VS), :] = rest

    def drain(self):
        for ref, sem in ((self.over_x, 0), (self.over_y, 1), (self.after_x, 2), (self.after_y, 3), (self.passing, 4)):
            self.copy(ref, ref, sem, self.place.far(True)).wait_send()


PROGRAM = (
    ("gather", 0),
    ("gather", 1),
    ("gather", 2),
    ("group", 0),
    ("group", 1),
    ("group", 2),
    ("group", 3),
    ("group", 4),
    ("gather", 0),
    ("gather", 1),
    ("gather", 0),
    ("gather", 2),
    ("gather", 0),
    ("gather", 1),
    ("gather", 0),
    ("gather", 2),
    ("gather", 0),
    ("select", 0),
    ("cross", 0, 0),
    ("cross", 0, 1),
    ("cross", 0, 2),
    ("cross", 0, 3),
    ("gather", 1),
    ("cross", 0, 4),
    ("lags", 0, 0),
    ("lags", 0, 1),
    ("gather", 2),
    ("lags", 0, 2),
    ("lags", 0, 3),
    ("gather", 1),
    ("relay", 0),
    ("gather", 2),
    ("gather", 1),
    ("after_x", 0),
    ("gather", 2),
    ("after_y", 0),
    ("gather", 1),
    ("select", 1),
    ("cross", 1, 0),
    ("gather", 2),
    ("cross", 1, 1),
    ("cross", 1, 2),
    ("cross", 1, 3),
    ("cross", 1, 4),
    ("lags", 1, 0),
    ("lags", 1, 1),
    ("lags", 1, 2),
    ("lags", 1, 3),
    ("select", 2),
    ("cross", 2, 0),
    ("cross", 2, 1),
    ("cross", 2, 2),
    ("cross", 2, 3),
    ("cross", 2, 4),
    ("lags", 2, 0),
    ("relay", 1),
    ("lags", 2, 1),
    ("lags", 2, 2),
    ("lags", 2, 3),
    ("relay", 2),
    ("final", 0),
    ("after_x", 1),
    ("after_y", 1),
    ("after_y", 2),
    ("after_x", 2),
    ("final", 1),
    ("final", 2),
)


def kernel(spectra, lag_table, pattern, slots, out, rb, turned, wide, crossed, spec, table, load, *rest):
    sums, (g_send, g_recv, r_send, r_recv), bufs = rest[:7], rest[7:11], rest[11:]
    loads = []
    for n in range(5):
        bins = pl.ds(n * 128, 128)
        loads.append(pltpu.make_async_copy(spectra.at[:, :, bins], spec.at[:, :, bins], load.at[n]))
    loads.append(pltpu.make_async_copy(lag_table, table, load.at[5]))
    for copy in loads:
        copy.start()
    place = Place()
    blk = place.blk
    barrier = pltpu.get_barrier_semaphore()
    peers = [place.near(True), place.near(flip_core=True)] + [place.near(dz=dz) for dz in (1, -1, 2, -2)]
    peers += [place.far(True)] + [place.far(dy=dy) for dy in (1, 2, 3)]
    for device in peers:
        pl.semaphore_signal(barrier, inc=1, device_id=device, device_id_type=MESH)

    def store(s, h, p, rows):
        for n, stage in enumerate(STAGES):
            if s in stage:
                own = 2 if KINDS[n] is Ring else OWN
                bufs[n][own, stage.index(s), h * NQ : (h + 1) * NQ, p * 128 : (p + 1) * 128] = rows

    own_sources(spec, turned, lambda n: loads[n].wait(), store)
    pl.semaphore_wait(barrier, len(peers))

    gathers = [KINDS[n](n, bufs[n], g_recv, g_send, place) for n in range(len(STAGES))]
    reduces = [Reduce(n, place, sums, r_send, r_recv) for n in range(len(STAGES))]
    steps = [iter(gather.steps()) for gather in gathers]

    def look(i, found):
        on = pattern[i, blk] > 0
        flip_x = jnp.abs(i // (2 * ZS) - place.xl)
        flip_core = jnp.abs(lax.rem(i, 2) - place.c)
        dz = lax.rem(lax.rem(i // 2, ZS) - place.z + ZS, ZS)
        slot = slots[i, blk]
        rule = [kind.index(flip_x, dz, flip_core) for kind in (Direct, Ring)]
        return tuple(
            tuple(jnp.where(on & (slot == k), at, old[k]) for k in range(SLOTS)) for at, old in zip(rule, found)
        )

    found = []

    def group(n):
        if not found:
            found.extend(lax.fori_loop(0, 4 * ZS, look, ((jnp.int32(-1),) * SLOTS,) * 2))
        group_receivers(spec, rb, n * 8, 8)

    def select(n):
        if n == 0:
            loads[5].wait()
        block = found[0 if KINDS[n] is Direct else 1]
        for k in range(SLOTS):
            present = jnp.where(block[k] >= 0, 1.0, 0.0)
            for si in range(len(STAGES[n])):
                rows = bufs[n][jnp.maximum(block[k], 0), si].astype(jnp.float32) * present
                for p in range(2):
                    wide[si, p, k] = rows[:, p * 128 : (p + 1) * 128]

    def lags(n, turn):
        for side in (1, 0):
            rows = crossed[place.slot(side == 1, TURNS[turn]), :, : 128 * len(STAGES[n])]
            got = jnp.dot(table[...], rows, preferred_element_type=jnp.float32).astype(jnp.bfloat16)
            for si, s in enumerate(STAGES[n]):
                sums[0][s, side, turn] = got[:, si * 128 : (si + 1) * 128]
        reduces[n].sent(turn)

    run = {
        "gather": lambda n: next(steps[n])(),
        "group": group,
        "select": select,
        "cross": lambda n, piece: cross(rb, wide, crossed, len(STAGES[n]), piece * 16, 16),
        "lags": lags,
        "relay": lambda n: reduces[n].relay(),
        "after_x": lambda n: reduces[n].combine_x(),
        "after_y": lambda n: reduces[n].combine_y(),
        "final": lambda s: reduces[s].final(out),
    }
    for name, *arguments in PROGRAM:
        run[name](*arguments)
    for gather in gathers:
        gather.drain()
    for reduce in reduces:
        reduce.drain()


def per_device(spectra, pattern, slot_of_pair, table):
    vmem = pl.BlockSpec(memory_space=pltpu.VMEM)
    smem = pl.BlockSpec(memory_space=pltpu.SMEM)
    hbm = pl.BlockSpec(memory_space=pl.ANY)
    stacks = pl.pallas_call(
        kernel,
        out_shape=jax.ShapeDtypeStruct((LAGS * VS, 128), jnp.float32),
        in_specs=[hbm, hbm, smem, smem],
        out_specs=vmem,
        scratch_shapes=[
            pltpu.VMEM((NG, 256, 128), jnp.bfloat16),
            pltpu.VMEM((2, 2, 2 * 128, 128), jnp.float32),
            pltpu.VMEM((MOST, 2, SLOTS, NG, 128), jnp.float32),
            pltpu.VMEM((SLOTS, 2 * F, 128 * MOST), jnp.bfloat16),
            pltpu.VMEM((2, WINDOWS // 8, F, 128), jnp.bfloat16),
            pltpu.VMEM((LAGS, 2 * F), jnp.bfloat16),
            pltpu.SemaphoreType.DMA((6,)),
            pltpu.VMEM((VS, 2, YS, LAGS, 128), jnp.bfloat16),
            pltpu.VMEM((VS, YS, FIRST, 128), jnp.bfloat16),
            pltpu.VMEM((VS, YS - 1, FIRST, 128), jnp.bfloat16),
            pltpu.VMEM((VS, 2, 2, 2, HALF, 128), jnp.bfloat16),
            pltpu.VMEM((VS, REST, 128), jnp.bfloat16),
            pltpu.VMEM((VS, REST, 128), jnp.bfloat16),
            pltpu.VMEM((VS, 2, 2, HALF, 128), jnp.bfloat16),
            pltpu.SemaphoreType.DMA((len(STAGES), 3)),
            pltpu.SemaphoreType.DMA((len(STAGES), 16)),
            pltpu.SemaphoreType.DMA((len(STAGES), 5)),
            pltpu.SemaphoreType.DMA((len(STAGES), 5)),
                ]
        + [pltpu.VMEM((4 * ZS, len(stage), NG, 256), jnp.bfloat16) for stage in STAGES],
        compiler_params=pltpu.CompilerParams(collective_id=0, has_side_effects=True, vmem_limit_bytes=56 << 20),
        name="correlate",
    )(spectra, table, pattern, slot_of_pair)
    return stacks.astype(jnp.bfloat16).reshape(1, LAGS, VS, 128)


def solution(mesh):
    mapped = jax.shard_map(
        per_device,
        mesh=mesh,
        in_specs=(P(None, "grp", None, "blk"), P(), P(), P()),
        out_specs=P("grp", None, None, "blk"),
        check_vma=False,
    )
    return lambda spectra, pattern, slot_of_pair: mapped(spectra, pattern, slot_of_pair, jnp.asarray(lag_rows()))
```

```python
import functools
import math

import jax
import jax.numpy as jnp
import ml_dtypes
import numpy as np
from jax import lax
from jax.experimental import pallas as pl
from jax.experimental.pallas import tpu as pltpu
from jax.sharding import PartitionSpec as P

F = 640
LAGS = 512
VS = 4
SLOTS = 8
WINDOWS = 128
NG = F // 8
ZS = 8
YS = 4
NQ = NG // 2
MESH = pl.DeviceIdType.MESH
FIRST = 256
REST = LAGS - FIRST
HALF = REST // 2


def lag_rows():
    bins = np.arange(F)
    shifts = np.arange(LAGS) - LAGS // 2
    angles = math.pi / F * (shifts[:, None] * bins[None, :] % (2 * F))
    factor = 1.0 / math.sqrt(2.0 * WINDOWS * F)
    both = np.stack([np.cos(angles), -np.sin(angles)], axis=1) * factor
    both = both.reshape(LAGS, 2, NQ, 2, 8).transpose(0, 3, 2, 1, 4)
    return both.reshape(LAGS, 2 * F).astype(ml_dtypes.bfloat16)


def group_receivers(spec, rb, first, count):
    def step(n, carry):
        q = first + n
        x = spec[:, :, pl.ds(pl.multiple_of(q * 16, 16), 16), :].astype(jnp.float32)
        rb[q] = x[:, :, :8, :].reshape(256, 128).astype(jnp.bfloat16)
        rb[NQ + q] = x[:, :, 8:, :].reshape(256, 128).astype(jnp.bfloat16)
        return carry

    lax.fori_loop(0, count, step, 0, unroll=2)


def own_sources(spec, turned, loaded, store):
    lane = lax.broadcasted_iota(jnp.int32, (8, 128), 1)
    for begin, count in ((0, 32), (32, NQ - 32)):

        def step(q, acc, begin=begin):
            x = spec[:, :, pl.ds(pl.multiple_of((begin + q) * 16, 16), 16), :].astype(jnp.float32)
            x = jnp.where(lane < VS, x.reshape(32, 2, 8, 128), 0.0).reshape(512, 128)
            return acc + pltpu.roll(x, q * VS, 1)

        acc = jnp.zeros((512, 128), jnp.float32)
        for chunk in range(count // 8):
            loaded(begin // 8 + chunk)
            acc = lax.fori_loop(chunk * 8, chunk * 8 + 8, step, acc, unroll=8)
        acc = acc.reshape(32, 2, 8, 128)
        for h in range(2):
            rows = acc[:, h].reshape(256, 128).T
            for p in range(2):
                turned[h, p, begin * VS : (begin + count) * VS, :] = rows[: count * VS, p * 128 : (p + 1) * 128]
    for s in range(VS):
        for h in range(2):
            for p in range(2):
                store(s, h, p, turned[h, p, pl.ds(s, NQ, stride=VS), :].astype(jnp.bfloat16))


def cross(rb, wide, crossed, count, first, groups):
    row = lax.broadcasted_iota(jnp.int32, (8, 128), 0)
    lane = lax.broadcasted_iota(jnp.int32, (8, 128), 1)
    mask = (lane % 8 == row).astype(jnp.float32)

    def step(n, carry):
        g = first + n
        left, right = [], []
        for si in range(count):
            for k in range(SLOTS):
                re = wide[si, 0, k, pl.ds(g, 1), :] * mask
                im = wide[si, 1, k, pl.ds(g, 1), :] * mask
                left.append(jnp.concatenate([re, im], 0).astype(jnp.bfloat16))
                right.append(jnp.concatenate([im, -re], 0).astype(jnp.bfloat16))
        rows = jnp.concatenate([jnp.concatenate(left, 0), jnp.concatenate(right, 0)], 1)
        got = jnp.dot(rows, rb[g], preferred_element_type=jnp.float32).astype(jnp.bfloat16)
        at = pl.multiple_of(g * 16, 16)
        for si in range(count):
            part = got[si * 128 : (si + 1) * 128].reshape(SLOTS, 16, 128)
            crossed[:, pl.ds(at, 16), si * 128 : (si + 1) * 128] = part
        return carry

    lax.fori_loop(0, groups, step, 0, unroll=40)


class Place:
    def __init__(self):
        blk, grp = lax.axis_index("blk"), lax.axis_index("grp")
        self.blk, self.grp = blk, grp
        self.xl, self.z, self.c = blk // (2 * ZS), lax.rem(blk // 2, ZS), lax.rem(blk, 2)
        self.xh, self.y = grp // YS, lax.rem(grp, YS)
        self.known = {}

    def once(self, key, make):
        if key not in self.known:
            self.known[key] = make()
        return self.known[key]

    def near(self, flip_x=False, dz=0, flip_core=False):
        xl = 1 - self.xl if flip_x else self.xl
        c = 1 - self.c if flip_core else self.c
        at = lambda: xl * (2 * ZS) + lax.rem(self.z + dz + ZS, ZS) * 2 + c
        if not isinstance(dz, int):
            return (at(), self.grp)
        return (self.once(("near", flip_x, dz, flip_core), at), self.grp)

    def slot(self, flip_x, dy):
        xh = 1 - self.xh if flip_x else self.xh
        return self.once(("slot", flip_x, dy), lambda: xh * YS + lax.rem(self.y + dy, YS))

    def far(self, flip_x=False, dy=0):
        return (self.blk, self.slot(flip_x, dy))


OWN = 2
X_SEND, CORE_SEND, Z_SEND = 0, 1, 2
CORE_RECV = 15


def at_z(dz, own=OWN):
    return (dz + own) % ZS


class Gather:
    def __init__(self, n, buf, recv, send, place):
        self.buf, self.recv, self.send, self.place = buf, recv.at[n], send.at[n], place

    def copy(self, src, dst, to, recv, send):
        return pltpu.make_async_remote_copy(
            src_ref=self.buf.at[pl.ds(*src)],
            dst_ref=self.buf.at[pl.ds(*dst)],
            send_sem=self.send.at[send],
            recv_sem=self.recv.at[recv],
            device_id=to,
            device_id_type=MESH,
        )

    def wait(self, blocks, recv):
        self.copy(blocks, blocks, self.place.near(True), recv, X_SEND).wait_recv()

    def to_core(self, first, count):
        self.copy((first, count), (2 * ZS + first, count), self.place.near(flip_core=True), CORE_RECV, CORE_SEND).start()

    def finish(self):
        self.wait((2 * ZS, 2 * ZS), CORE_RECV)

    def drain(self):
        for count, send in ((self.X_BLOCKS, X_SEND), (2 * ZS, CORE_SEND), (self.Z_BLOCKS, Z_SEND)):
            self.copy((0, count), (0, count), self.place.near(True), 0, send).wait_send()


class Ring(Gather):
    X_BLOCKS, Z_BLOCKS, OWN = 1, 14, 1

    @staticmethod
    def index(flip_x, dz, flip_core):
        return (flip_core * ZS + lax.rem(dz + 1, ZS)) * 2 + flip_x

    def start(self):
        self.copy((2, 1), (3, 1), self.place.near(True), 0, X_SEND).start()

    def partner(self):
        self.wait((3, 1), 0)
        for sign, first in ((1, 1), (-1, 5)):
            self.copy((2, 2), (2 * at_z(-sign, 1), 2), self.place.near(dz=sign), first, Z_SEND).start()

    def hop(self, h):
        for sign, first in ((1, 0), (-1, 4)):
            single = 0 if sign > 0 else 1
            here, there = 2 * at_z(-h * sign, 1), 2 * at_z(-(h + 1) * sign, 1)
            blocks = (here, 2) if h < 4 else (here + single, 1)
            self.wait(blocks, first + h)
            ahead = self.place.near(dz=sign)
            if h < 3:
                self.copy(blocks, (there, 2), ahead, first + h + 1, Z_SEND).start()
            elif h == 3:
                self.copy((here + single, 1), (there + single, 1), ahead, first + 4, Z_SEND).start()
        for blocks in {1: ((0, 6),), 3: ((6, 4), (12, 4)), 4: ((10, 2),)}.get(h, ()):
            self.to_core(*blocks)

    def steps(self):
        return [self.start, self.partner] + [functools.partial(self.hop, h) for h in (1, 2, 3, 4)] + [self.finish]


class Direct(Gather):
    X_BLOCKS, Z_BLOCKS = 8, 7
    NEAR, FAR = (0, 5), (5, 3)

    @staticmethod
    def index(flip_x, dz, flip_core):
        return (flip_core * 2 + flip_x) * ZS + lax.rem(dz + OWN, ZS)

    def start(self):
        for dz in (1, -1, 2, -2):
            self.copy((OWN, 1), (at_z(-dz), 1), self.place.near(dz=dz), 0, Z_SEND).start()

    def onward(self, blocks, recv):
        first, count = blocks
        self.copy(blocks, (ZS + first, count), self.place.near(True), recv, X_SEND).start()
        self.to_core(*blocks)

    def second(self):
        place = self.place
        self.wait((0, 4), 0)
        for sign in (1, -1):
            self.copy((at_z(-2 * sign), 1), (at_z(-3 * sign), 1), place.near(dz=sign), 1, Z_SEND).start()
        sign = 1 - 2 * place.c
        self.copy((OWN - 2 * sign, 1), (at_z(4), 1), place.near(dz=2 * sign), 1, Z_SEND).start()
        self.onward(self.NEAR, 2)

    def third(self):
        self.wait(self.FAR, 1)
        self.onward(self.FAR, 3)

    def from_x(self, blocks, recv):
        first, count = blocks
        self.wait((ZS + first, count), recv)
        self.to_core(ZS + first, count)

    def steps(self):
        return [
            self.start,
            self.second,
            self.third,
            lambda: self.from_x(self.NEAR, 2),
            lambda: self.from_x(self.FAR, 3),
            self.finish,
        ]


STAGES = ((0,), (1, 2), (3,))
KINDS = (Direct, Ring, Ring)
MOST = max(len(stage) for stage in STAGES)
TURNS = (2, 1, 3, 0)


class Reduce:
    def __init__(self, n, place, bufs, send, recv):
        self.stage, self.place = STAGES[n], place
        part = pl.ds(STAGES[n][0], len(STAGES[n]))
        refs = (buf.at[part] for buf in bufs)
        self.parts, self.over_x, self.after_x, self.over_y, self.side, self.after_y, self.passing = refs
        self.send, self.recv = send.at[n], recv.at[n]

    def copy(self, src, dst, sem, to):
        return pltpu.make_async_remote_copy(
            src_ref=src,
            dst_ref=dst,
            send_sem=self.send.at[sem],
            recv_sem=self.recv.at[sem],
            device_id=to,
            device_id_type=MESH,
        )

    def sent(self, turn):
        if turn % 2:
            two = pl.ds(turn - 1, 2)
            src = self.parts.at[:, 1, two, pl.ds(0, FIRST)]
            self.copy(src, self.over_x.at[:, two], 0, self.place.far(True)).start()
        if turn == 0:
            for half, dy in ((0, 1), (1, 3)):
                src = self.parts.at[:, :, 0, pl.ds(FIRST + half * HALF, HALF)]
                self.copy(src, self.passing.at[:, :, half], 4, self.place.far(dy=dy)).start()
        elif turn < YS - 1:
            self.along(turn, turn % 2)

    def along(self, turn, half):
        rows = pl.ds(FIRST + half * HALF, HALF)
        to = self.place.far(dy=TURNS[turn])
        self.copy(self.parts.at[:, :, turn, rows], self.over_y.at[:, turn - 1, :, half], 1, to).start()

    def relay(self):
        self.wait(self.passing, 4)
        for half in range(2):
            begin = FIRST + half * HALF
            for si in range(len(self.stage)):
                for side in range(2):
                    own = self.parts[si, side, 1 + half, begin : begin + HALF].astype(jnp.float32)
                    own += self.passing[si, side, half].astype(jnp.float32)
                    self.parts[si, side, 1 + half, begin : begin + HALF] = own.astype(jnp.bfloat16)
            self.along(1 + half, half)

    def wait(self, ref, sem):
        self.copy(ref, ref, sem, self.place.far(True)).wait_recv()

    def combine_x(self):
        self.wait(self.over_x, 0)
        for turn in range(YS - 1):
            for si in range(len(self.stage)):
                own = self.parts[si, 0, turn, :FIRST].astype(jnp.float32)
                self.over_x[si, turn] = (own + self.over_x[si, turn].astype(jnp.float32)).astype(jnp.bfloat16)
            self.copy(self.over_x.at[:, turn], self.after_x.at[:, turn], 2, self.place.far(dy=TURNS[turn])).start()

    def along_y(self, si, side):
        total = self.parts[si, side, YS - 1, FIRST:].astype(jnp.float32)
        for m in range(2):
            total += self.over_y[si, m, side].astype(jnp.float32).reshape(REST, 128)
        return total

    def combine_y(self):
        self.wait(self.over_y, 1)
        for si in range(len(self.stage)):
            self.side[si] = self.along_y(si, 1).astype(jnp.bfloat16)
        self.copy(self.side, self.after_y, 3, self.place.far(True)).start()

    def final(self, out):
        rest = [self.along_y(si, 0) for si in range(len(self.stage))]
        self.wait(self.after_x, 2)
        for si, s in enumerate(self.stage):
            total = self.parts[si, 0, YS - 1, :FIRST].astype(jnp.float32)
            total += self.over_x[si, YS - 1].astype(jnp.float32)
            for turn in range(YS - 1):
                total += self.after_x[si, turn].astype(jnp.float32)
            out[pl.ds(s, FIRST, stride=VS), :] = total
        self.wait(self.after_y, 3)
        for si, s in enumerate(self.stage):
            last = rest[si] + self.after_y[si].astype(jnp.float32)
            out[pl.ds(FIRST * VS + s, REST, stride=VS), :] = last

    def drain(self):
        for ref, sem in ((self.over_x, 0), (self.over_y, 1), (self.after_x, 2), (self.after_y, 3), (self.passing, 4)):
            self.copy(ref, ref, sem, self.place.far(True)).wait_send()


PROGRAM = (
    ("gather", 0),
    ("gather", 1),
    ("gather", 2),
    ("group", 0),
    ("group", 1),
    ("group", 2),
    ("group", 3),
    ("group", 4),
    ("gather", 0),
    ("gather", 1),
    ("gather", 0),
    ("gather", 2),
    ("gather", 0),
    ("gather", 1),
    ("gather", 0),
    ("gather", 2),
    ("gather", 0),
    ("select", 0),
    ("cross", 0, 0),
    ("cross", 0, 1),
    ("cross", 0, 2),
    ("cross", 0, 3),
    ("gather", 1),
    ("cross", 0, 4),
    ("lags", 0, 0),
    ("lags", 0, 1),
    ("gather", 2),
    ("lags", 0, 2),
    ("lags", 0, 3),
    ("gather", 1),
    ("relay", 0),
    ("gather", 2),
    ("gather", 1),
    ("after_x", 0),
    ("gather", 2),
    ("after_y", 0),
    ("gather", 1),
    ("select", 1),
    ("cross", 1, 0),
    ("gather", 2),
    ("cross", 1, 1),
    ("cross", 1, 2),
    ("cross", 1, 3),
    ("cross", 1, 4),
    ("lags", 1, 0),
    ("lags", 1, 1),
    ("lags", 1, 2),
    ("lags", 1, 3),
    ("select", 2),
    ("cross", 2, 0),
    ("cross", 2, 1),
    ("cross", 2, 2),
    ("cross", 2, 3),
    ("cross", 2, 4),
    ("lags", 2, 0),
    ("relay", 1),
    ("lags", 2, 1),
    ("lags", 2, 2),
    ("lags", 2, 3),
    ("relay", 2),
    ("final", 0),
    ("after_x", 1),
    ("after_y", 1),
    ("after_y", 2),
    ("after_x", 2),
    ("final", 1),
    ("final", 2),
)


def kernel(spectra, lag_table, pattern, slots, out, rb, turned, wide, crossed, spec, table, stacked, load, *rest):
    sums, (g_send, g_recv, r_send, r_recv), bufs = rest[:7], rest[7:11], rest[11:]
    loads = []
    for n in range(5):
        bins = pl.ds(n * 128, 128)
        loads.append(pltpu.make_async_copy(spectra.at[:, :, bins], spec.at[:, :, bins], load.at[n]))
    loads.append(pltpu.make_async_copy(lag_table, table, load.at[5]))
    for copy in loads:
        copy.start()
    place = Place()
    blk = place.blk
    barrier = pltpu.get_barrier_semaphore()
    peers = [place.near(True), place.near(flip_core=True)] + [place.near(dz=dz) for dz in (1, -1, 2, -2)]
    peers += [place.far(True)] + [place.far(dy=dy) for dy in (1, 2, 3)]
    for device in peers:
        pl.semaphore_signal(barrier, inc=1, device_id=device, device_id_type=MESH)

    def store(s, h, p, rows):
        for n, stage in enumerate(STAGES):
            if s in stage:
                own = 2 if KINDS[n] is Ring else OWN
                bufs[n][own, stage.index(s), h * NQ : (h + 1) * NQ, p * 128 : (p + 1) * 128] = rows

    own_sources(spec, turned, lambda n: loads[n].wait(), store)
    pl.semaphore_wait(barrier, len(peers))

    gathers = [KINDS[n](n, bufs[n], g_recv, g_send, place) for n in range(len(STAGES))]
    reduces = [Reduce(n, place, sums, r_send, r_recv) for n in range(len(STAGES))]
    steps = [iter(gather.steps()) for gather in gathers]

    def look(i, found):
        on = pattern[i, blk] > 0
        flip_x = jnp.abs(i // (2 * ZS) - place.xl)
        flip_core = jnp.abs(lax.rem(i, 2) - place.c)
        dz = lax.rem(lax.rem(i // 2, ZS) - place.z + ZS, ZS)
        slot = slots[i, blk]
        rule = [kind.index(flip_x, dz, flip_core) for kind in (Direct, Ring)]
        return tuple(
            tuple(jnp.where(on & (slot == k), at, old[k]) for k in range(SLOTS)) for at, old in zip(rule, found)
        )

    found = []

    def group(n):
        if not found:
            found.extend(lax.fori_loop(0, 4 * ZS, look, ((jnp.int32(-1),) * SLOTS,) * 2))
        group_receivers(spec, rb, n * 8, 8)

    def select(n):
        if n == 0:
            loads[5].wait()
        block = found[0 if KINDS[n] is Direct else 1]
        for k in range(SLOTS):
            present = jnp.where(block[k] >= 0, 1.0, 0.0)
            for si in range(len(STAGES[n])):
                rows = bufs[n][jnp.maximum(block[k], 0), si].astype(jnp.float32) * present
                for p in range(2):
                    wide[si, p, k] = rows[:, p * 128 : (p + 1) * 128]

    def lags(n, turn):
        for side in (1, 0):
            rows = crossed[place.slot(side == 1, TURNS[turn]), :, : 128 * len(STAGES[n])]
            got = jnp.dot(table[...], rows, preferred_element_type=jnp.float32).astype(jnp.bfloat16)
            for si, s in enumerate(STAGES[n]):
                sums[0][s, side, turn] = got[:, si * 128 : (si + 1) * 128]
        reduces[n].sent(turn)

    run = {
        "gather": lambda n: next(steps[n])(),
        "group": group,
        "select": select,
        "cross": lambda n, piece: cross(rb, wide, crossed, len(STAGES[n]), piece * 20, 40) if piece % 2 == 0 and piece < 4 else None,
        "lags": lags,
        "relay": lambda n: reduces[n].relay(),
        "after_x": lambda n: reduces[n].combine_x(),
        "after_y": lambda n: reduces[n].combine_y(),
        "final": lambda s: reduces[s].final(stacked),
    }
    for name, *arguments in PROGRAM:
        run[name](*arguments)
    out[...] = stacked[...].astype(jnp.bfloat16)
    for gather in gathers:
        gather.drain()
    for reduce in reduces:
        reduce.drain()


def hand_on(source, target):
    target[...] = source[...]


def per_device(spectra, pattern, slot_of_pair, table):
    vmem = pl.BlockSpec(memory_space=pltpu.VMEM)
    smem = pl.BlockSpec(memory_space=pltpu.SMEM)
    hbm = pl.BlockSpec(memory_space=pl.ANY)
    stacks = pl.pallas_call(
        kernel,
        out_shape=jax.ShapeDtypeStruct((LAGS * VS, 128), jnp.bfloat16),
        in_specs=[hbm, hbm, smem, smem],
        out_specs=vmem,
        scratch_shapes=[
            pltpu.VMEM((NG, 256, 128), jnp.bfloat16),
            pltpu.VMEM((2, 2, 2 * 128, 128), jnp.float32),
            pltpu.VMEM((MOST, 2, SLOTS, NG, 128), jnp.float32),
            pltpu.VMEM((SLOTS, 2 * F, 128 * MOST), jnp.bfloat16),
            pltpu.VMEM((2, WINDOWS // 8, F, 128), jnp.bfloat16),
            pltpu.VMEM((LAGS, 2 * F), jnp.bfloat16),
            pltpu.VMEM((LAGS * VS, 128), jnp.float32),
            pltpu.SemaphoreType.DMA((6,)),
            pltpu.VMEM((VS, 2, YS, LAGS, 128), jnp.bfloat16),
            pltpu.VMEM((VS, YS, FIRST, 128), jnp.bfloat16),
            pltpu.VMEM((VS, YS - 1, FIRST, 128), jnp.bfloat16),
            pltpu.VMEM((VS, 2, 2, 2, HALF, 128), jnp.bfloat16),
            pltpu.VMEM((VS, REST, 128), jnp.bfloat16),
            pltpu.VMEM((VS, REST, 128), jnp.bfloat16),
            pltpu.VMEM((VS, 2, 2, HALF, 128), jnp.bfloat16),
            pltpu.SemaphoreType.DMA((len(STAGES), 3)),
            pltpu.SemaphoreType.DMA((len(STAGES), 16)),
            pltpu.SemaphoreType.DMA((len(STAGES), 5)),
            pltpu.SemaphoreType.DMA((len(STAGES), 5)),
                ]
        + [pltpu.VMEM((4 * ZS, len(stage), NG, 256), jnp.bfloat16) for stage in STAGES],
        compiler_params=pltpu.CompilerParams(collective_id=0, has_side_effects=True, vmem_limit_bytes=56 << 20),
        name="correlate",
    )(spectra, table, pattern, slot_of_pair)
    stacks = pl.pallas_call(
        hand_on,
        out_shape=jax.ShapeDtypeStruct(stacks.shape, stacks.dtype),
        in_specs=[vmem],
        out_specs=vmem,
        name="hand_on",
    )(stacks)
    return stacks.reshape(1, LAGS, VS, 128)


def solution(mesh):
    mapped = jax.shard_map(
        per_device,
        mesh=mesh,
        in_specs=(P(None, "grp", None, "blk"), P(), P(), P()),
        out_specs=P("grp", None, None, "blk"),
        check_vma=False,
    )
    return lambda spectra, pattern, slot_of_pair: mapped(spectra, pattern, slot_of_pair, jnp.asarray(lag_rows()))
```

```python
import functools
import math

import jax
import jax.numpy as jnp
import ml_dtypes
import numpy as np
from jax import lax
from jax.experimental import pallas as pl
from jax.experimental.pallas import tpu as pltpu
from jax.sharding import PartitionSpec as P

F = 640
LAGS = 512
VS = 4
SLOTS = 8
WINDOWS = 128
NG = F // 8
ZS = 8
YS = 4
NQ = NG // 2
MESH = pl.DeviceIdType.MESH
FIRST = 256
REST = LAGS - FIRST
HALF = REST // 2


def lag_rows():
    bins = np.arange(F)
    shifts = np.arange(LAGS) - LAGS // 2
    angles = math.pi / F * (shifts[:, None] * bins[None, :] % (2 * F))
    factor = 1.0 / math.sqrt(2.0 * WINDOWS * F)
    both = np.stack([np.cos(angles), -np.sin(angles)], axis=1) * factor
    both = both.reshape(LAGS, 2, NQ, 2, 8).transpose(0, 3, 2, 1, 4)
    return both.reshape(LAGS, 2 * F).astype(ml_dtypes.bfloat16)


def group_receivers(spec, rb, first, count):
    def step(n, carry):
        q = first + n
        x = spec[:, :, pl.ds(pl.multiple_of(q * 16, 16), 16), :].astype(jnp.float32)
        rb[q] = x[:, :, :8, :].reshape(256, 128).astype(jnp.bfloat16)
        rb[NQ + q] = x[:, :, 8:, :].reshape(256, 128).astype(jnp.bfloat16)
        return carry

    lax.fori_loop(0, count, step, 0, unroll=2)


def own_sources(spec, turned, loaded, store):
    lane = lax.broadcasted_iota(jnp.int32, (8, 128), 1)
    for begin, count in ((0, 32), (32, NQ - 32)):

        def step(q, acc, begin=begin):
            x = spec[:, :, pl.ds(pl.multiple_of((begin + q) * 16, 16), 16), :].astype(jnp.float32)
            x = jnp.where(lane < VS, x.reshape(32, 2, 8, 128), 0.0).reshape(512, 128)
            return acc + pltpu.roll(x, q * VS, 1)

        acc = jnp.zeros((512, 128), jnp.float32)
        for chunk in range(count // 8):
            loaded(begin // 8 + chunk)
            acc = lax.fori_loop(chunk * 8, chunk * 8 + 8, step, acc, unroll=8)
        acc = acc.reshape(32, 2, 8, 128)
        for h in range(2):
            rows = acc[:, h].reshape(256, 128).T
            for p in range(2):
                turned[h, p, begin * VS : (begin + count) * VS, :] = rows[: count * VS, p * 128 : (p + 1) * 128]
    for s in range(VS):
        for h in range(2):
            for p in range(2):
                store(s, h, p, turned[h, p, pl.ds(s, NQ, stride=VS), :].astype(jnp.bfloat16))


def cross(rb, wide, crossed, count, first, groups):
    row = lax.broadcasted_iota(jnp.int32, (8, 128), 0)
    lane = lax.broadcasted_iota(jnp.int32, (8, 128), 1)
    mask = (lane % 8 == row).astype(jnp.float32)

    def step(n, carry):
        g = first + n
        left, right = [], []
        for si in range(count):
            for k in range(SLOTS):
                re = wide[si, 0, k, pl.ds(g, 1), :] * mask
                im = wide[si, 1, k, pl.ds(g, 1), :] * mask
                left.append(jnp.concatenate([re, im], 0).astype(jnp.bfloat16))
                right.append(jnp.concatenate([im, -re], 0).astype(jnp.bfloat16))
        rows = jnp.concatenate([jnp.concatenate(left, 0), jnp.concatenate(right, 0)], 1)
        got = jnp.dot(rows, rb[g], preferred_element_type=jnp.float32).astype(jnp.bfloat16)
        at = pl.multiple_of(g * 16, 16)
        for si in range(count):
            part = got[si * 128 : (si + 1) * 128].reshape(SLOTS, 16, 128)
            crossed[:, pl.ds(at, 16), si * 128 : (si + 1) * 128] = part
        return carry

    lax.fori_loop(0, groups, step, 0, unroll=40)


class Place:
    def __init__(self):
        blk, grp = lax.axis_index("blk"), lax.axis_index("grp")
        self.blk, self.grp = blk, grp
        self.xl, self.z, self.c = blk // (2 * ZS), lax.rem(blk // 2, ZS), lax.rem(blk, 2)
        self.xh, self.y = grp // YS, lax.rem(grp, YS)
        self.known = {}

    def once(self, key, make):
        if key not in self.known:
            self.known[key] = make()
        return self.known[key]

    def near(self, flip_x=False, dz=0, flip_core=False):
        xl = 1 - self.xl if flip_x else self.xl
        c = 1 - self.c if flip_core else self.c
        at = lambda: xl * (2 * ZS) + lax.rem(self.z + dz + ZS, ZS) * 2 + c
        if not isinstance(dz, int):
            return (at(), self.grp)
        return (self.once(("near", flip_x, dz, flip_core), at), self.grp)

    def slot(self, flip_x, dy):
        xh = 1 - self.xh if flip_x else self.xh
        return self.once(("slot", flip_x, dy), lambda: xh * YS + lax.rem(self.y + dy, YS))

    def far(self, flip_x=False, dy=0):
        return (self.blk, self.slot(flip_x, dy))


OWN = 2
X_SEND, CORE_SEND, Z_SEND = 0, 1, 2
CORE_RECV = 15


def at_z(dz, own=OWN):
    return (dz + own) % ZS


class Gather:
    def __init__(self, n, buf, recv, send, place):
        self.buf, self.recv, self.send, self.place = buf, recv.at[n], send.at[n], place

    def copy(self, src, dst, to, recv, send):
        return pltpu.make_async_remote_copy(
            src_ref=self.buf.at[pl.ds(*src)],
            dst_ref=self.buf.at[pl.ds(*dst)],
            send_sem=self.send.at[send],
            recv_sem=self.recv.at[recv],
            device_id=to,
            device_id_type=MESH,
        )

    def wait(self, blocks, recv):
        self.copy(blocks, blocks, self.place.near(True), recv, X_SEND).wait_recv()

    def to_core(self, first, count):
        self.copy((first, count), (2 * ZS + first, count), self.place.near(flip_core=True), CORE_RECV, CORE_SEND).start()

    def finish(self):
        self.wait((2 * ZS, 2 * ZS), CORE_RECV)

    def drain(self):
        for count, send in ((self.X_BLOCKS, X_SEND), (2 * ZS, CORE_SEND), (self.Z_BLOCKS, Z_SEND)):
            self.copy((0, count), (0, count), self.place.near(True), 0, send).wait_send()


class Ring(Gather):
    X_BLOCKS, Z_BLOCKS, OWN = 1, 14, 1

    @staticmethod
    def index(flip_x, dz, flip_core):
        return (flip_core * ZS + lax.rem(dz + 1, ZS)) * 2 + flip_x

    def start(self):
        self.copy((2, 1), (3, 1), self.place.near(True), 0, X_SEND).start()

    def partner(self):
        self.wait((3, 1), 0)
        for sign, first in ((1, 1), (-1, 5)):
            self.copy((2, 2), (2 * at_z(-sign, 1), 2), self.place.near(dz=sign), first, Z_SEND).start()

    def hop(self, h):
        for sign, first in ((1, 0), (-1, 4)):
            single = 0 if sign > 0 else 1
            here, there = 2 * at_z(-h * sign, 1), 2 * at_z(-(h + 1) * sign, 1)
            blocks = (here, 2) if h < 4 else (here + single, 1)
            self.wait(blocks, first + h)
            ahead = self.place.near(dz=sign)
            if h < 3:
                self.copy(blocks, (there, 2), ahead, first + h + 1, Z_SEND).start()
            elif h == 3:
                self.copy((here + single, 1), (there + single, 1), ahead, first + 4, Z_SEND).start()
        for blocks in {1: ((0, 6),), 3: ((6, 4), (12, 4)), 4: ((10, 2),)}.get(h, ()):
            self.to_core(*blocks)

    def steps(self):
        return [self.start, self.partner] + [functools.partial(self.hop, h) for h in (1, 2, 3, 4)] + [self.finish]


class Direct(Gather):
    X_BLOCKS, Z_BLOCKS = 8, 7
    NEAR, FAR = (0, 5), (5, 3)

    @staticmethod
    def index(flip_x, dz, flip_core):
        return (flip_core * 2 + flip_x) * ZS + lax.rem(dz + OWN, ZS)

    def start(self):
        for dz in (1, -1, 2, -2):
            self.copy((OWN, 1), (at_z(-dz), 1), self.place.near(dz=dz), 0, Z_SEND).start()

    def onward(self, blocks, recv):
        first, count = blocks
        self.copy(blocks, (ZS + first, count), self.place.near(True), recv, X_SEND).start()
        self.to_core(*blocks)

    def second(self):
        place = self.place
        self.wait((0, 4), 0)
        for sign in (1, -1):
            self.copy((at_z(-2 * sign), 1), (at_z(-3 * sign), 1), place.near(dz=sign), 1, Z_SEND).start()
        sign = 1 - 2 * place.c
        self.copy((OWN - 2 * sign, 1), (at_z(4), 1), place.near(dz=2 * sign), 1, Z_SEND).start()
        self.onward(self.NEAR, 2)

    def third(self):
        self.wait(self.FAR, 1)
        self.onward(self.FAR, 3)

    def from_x(self, blocks, recv):
        first, count = blocks
        self.wait((ZS + first, count), recv)
        self.to_core(ZS + first, count)

    def steps(self):
        return [
            self.start,
            self.second,
            self.third,
            lambda: self.from_x(self.NEAR, 2),
            lambda: self.from_x(self.FAR, 3),
            self.finish,
        ]


STAGES = ((0,), (1, 2), (3,))
KINDS = (Direct, Ring, Ring)
MOST = max(len(stage) for stage in STAGES)
TURNS = (2, 1, 3, 0)


class Reduce:
    def __init__(self, n, place, bufs, send, recv):
        self.stage, self.place = STAGES[n], place
        part = pl.ds(STAGES[n][0], len(STAGES[n]))
        refs = (buf.at[part] for buf in bufs)
        self.parts, self.over_x, self.after_x, self.over_y, self.side, self.after_y, self.passing = refs
        self.send, self.recv = send.at[n], recv.at[n]

    def copy(self, src, dst, sem, to):
        return pltpu.make_async_remote_copy(
            src_ref=src,
            dst_ref=dst,
            send_sem=self.send.at[sem],
            recv_sem=self.recv.at[sem],
            device_id=to,
            device_id_type=MESH,
        )

    def sent(self, turn):
        if turn % 2:
            two = pl.ds(turn - 1, 2)
            src = self.parts.at[:, 1, two, pl.ds(0, FIRST)]
            self.copy(src, self.over_x.at[:, two], 0, self.place.far(True)).start()
        if turn == 0:
            for half, dy in ((0, 1), (1, 3)):
                src = self.parts.at[:, :, 0, pl.ds(FIRST + half * HALF, HALF)]
                self.copy(src, self.passing.at[:, :, half], 4, self.place.far(dy=dy)).start()
        elif turn < YS - 1:
            self.along(turn, turn % 2)

    def along(self, turn, half):
        rows = pl.ds(FIRST + half * HALF, HALF)
        to = self.place.far(dy=TURNS[turn])
        self.copy(self.parts.at[:, :, turn, rows], self.over_y.at[:, turn - 1, :, half], 1, to).start()

    def relay(self):
        self.wait(self.passing, 4)
        for half in range(2):
            begin = FIRST + half * HALF
            for si in range(len(self.stage)):
                for side in range(2):
                    own = self.parts[si, side, 1 + half, begin : begin + HALF].astype(jnp.float32)
                    own += self.passing[si, side, half].astype(jnp.float32)
                    self.parts[si, side, 1 + half, begin : begin + HALF] = own.astype(jnp.bfloat16)
            self.along(1 + half, half)

    def wait(self, ref, sem):
        self.copy(ref, ref, sem, self.place.far(True)).wait_recv()

    def combine_x(self):
        self.wait(self.over_x, 0)
        for turn in range(YS - 1):
            for si in range(len(self.stage)):
                own = self.parts[si, 0, turn, :FIRST].astype(jnp.float32)
                self.over_x[si, turn] = (own + self.over_x[si, turn].astype(jnp.float32)).astype(jnp.bfloat16)
            self.copy(self.over_x.at[:, turn], self.after_x.at[:, turn], 2, self.place.far(dy=TURNS[turn])).start()

    def along_y(self, si, side):
        total = self.parts[si, side, YS - 1, FIRST:].astype(jnp.float32)
        for m in range(2):
            total += self.over_y[si, m, side].astype(jnp.float32).reshape(REST, 128)
        return total

    def combine_y(self):
        self.wait(self.over_y, 1)
        for si in range(len(self.stage)):
            self.side[si] = self.along_y(si, 1).astype(jnp.bfloat16)
        self.copy(self.side, self.after_y, 3, self.place.far(True)).start()

    def final(self, out):
        rest = [self.along_y(si, 0) for si in range(len(self.stage))]
        self.wait(self.after_x, 2)
        for si, s in enumerate(self.stage):
            total = self.parts[si, 0, YS - 1, :FIRST].astype(jnp.float32)
            total += self.over_x[si, YS - 1].astype(jnp.float32)
            for turn in range(YS - 1):
                total += self.after_x[si, turn].astype(jnp.float32)
            out[pl.ds(s, FIRST, stride=VS), :] = total
        self.wait(self.after_y, 3)
        for si, s in enumerate(self.stage):
            last = rest[si] + self.after_y[si].astype(jnp.float32)
            out[pl.ds(FIRST * VS + s, REST, stride=VS), :] = last

    def drain(self):
        for ref, sem in ((self.over_x, 0), (self.over_y, 1), (self.after_x, 2), (self.after_y, 3), (self.passing, 4)):
            self.copy(ref, ref, sem, self.place.far(True)).wait_send()


PROGRAM = (
    ("gather", 0),
    ("gather", 1),
    ("gather", 2),
    ("group", 0),
    ("group", 1),
    ("group", 2),
    ("group", 3),
    ("group", 4),
    ("gather", 0),
    ("gather", 1),
    ("gather", 0),
    ("gather", 2),
    ("gather", 0),
    ("gather", 1),
    ("gather", 0),
    ("gather", 2),
    ("gather", 0),
    ("select", 0),
    ("cross", 0, 0),
    ("cross", 0, 1),
    ("cross", 0, 2),
    ("cross", 0, 3),
    ("gather", 1),
    ("cross", 0, 4),
    ("lags", 0, 0),
    ("lags", 0, 1),
    ("gather", 2),
    ("lags", 0, 2),
    ("lags", 0, 3),
    ("gather", 1),
    ("relay", 0),
    ("gather", 2),
    ("gather", 1),
    ("after_x", 0),
    ("gather", 2),
    ("after_y", 0),
    ("gather", 1),
    ("select", 1),
    ("cross", 1, 0),
    ("gather", 2),
    ("cross", 1, 1),
    ("cross", 1, 2),
    ("cross", 1, 3),
    ("cross", 1, 4),
    ("lags", 1, 0),
    ("lags", 1, 1),
    ("lags", 1, 2),
    ("lags", 1, 3),
    ("select", 2),
    ("cross", 2, 0),
    ("cross", 2, 1),
    ("cross", 2, 2),
    ("cross", 2, 3),
    ("cross", 2, 4),
    ("lags", 2, 0),
    ("relay", 1),
    ("lags", 2, 1),
    ("lags", 2, 2),
    ("lags", 2, 3),
    ("relay", 2),
    ("final", 0),
    ("after_x", 1),
    ("after_y", 1),
    ("after_y", 2),
    ("after_x", 2),
    ("final", 1),
    ("final", 2),
)


def kernel(spectra, lag_table, pattern, slots, out, rb, turned, wide, crossed, spec, table, stacked, load, *rest):
    sums, (g_send, g_recv, r_send, r_recv), bufs = rest[:7], rest[7:11], rest[11:]
    loads = []
    for n in range(5):
        bins = pl.ds(n * 128, 128)
        loads.append(pltpu.make_async_copy(spectra.at[:, :, bins], spec.at[:, :, bins], load.at[n]))
    loads.append(pltpu.make_async_copy(lag_table, table, load.at[5]))
    for copy in loads:
        copy.start()
    place = Place()
    blk = place.blk
    barrier = pltpu.get_barrier_semaphore()
    peers = [place.near(True), place.near(flip_core=True)] + [place.near(dz=dz) for dz in (1, -1, 2, -2)]
    peers += [place.far(True)] + [place.far(dy=dy) for dy in (1, 2, 3)]
    for device in peers:
        pl.semaphore_signal(barrier, inc=1, device_id=device, device_id_type=MESH)

    def store(s, h, p, rows):
        for n, stage in enumerate(STAGES):
            if s in stage:
                own = 2 if KINDS[n] is Ring else OWN
                bufs[n][own, stage.index(s), h * NQ : (h + 1) * NQ, p * 128 : (p + 1) * 128] = rows

    own_sources(spec, turned, lambda n: loads[n].wait(), store)
    pl.semaphore_wait(barrier, len(peers))

    gathers = [KINDS[n](n, bufs[n], g_recv, g_send, place) for n in range(len(STAGES))]
    reduces = [Reduce(n, place, sums, r_send, r_recv) for n in range(len(STAGES))]
    steps = [iter(gather.steps()) for gather in gathers]

    def look(i, found):
        on = pattern[i, blk] > 0
        flip_x = jnp.abs(i // (2 * ZS) - place.xl)
        flip_core = jnp.abs(lax.rem(i, 2) - place.c)
        dz = lax.rem(lax.rem(i // 2, ZS) - place.z + ZS, ZS)
        slot = slots[i, blk]
        rule = [kind.index(flip_x, dz, flip_core) for kind in (Direct, Ring)]
        return tuple(
            tuple(jnp.where(on & (slot == k), at, old[k]) for k in range(SLOTS)) for at, old in zip(rule, found)
        )

    found = []

    def group(n):
        if not found:
            found.extend(lax.fori_loop(0, 4 * ZS, look, ((jnp.int32(-1),) * SLOTS,) * 2))
        group_receivers(spec, rb, n * 8, 8)

    def select(n):
        if n == 0:
            loads[5].wait()
        block = found[0 if KINDS[n] is Direct else 1]
        for k in range(SLOTS):
            present = jnp.where(block[k] >= 0, 1.0, 0.0)
            for si in range(len(STAGES[n])):
                rows = bufs[n][jnp.maximum(block[k], 0), si].astype(jnp.float32) * present
                for p in range(2):
                    wide[si, p, k] = rows[:, p * 128 : (p + 1) * 128]

    def lags(n, turn):
        for side in (1, 0):
            rows = crossed[place.slot(side == 1, TURNS[turn]), :, : 128 * len(STAGES[n])]
            got = jnp.dot(table[...], rows, preferred_element_type=jnp.float32).astype(jnp.bfloat16)
            for si, s in enumerate(STAGES[n]):
                sums[0][s, side, turn] = got[:, si * 128 : (si + 1) * 128]
        reduces[n].sent(turn)

    run = {
        "gather": lambda n: next(steps[n])(),
        "group": group,
        "select": select,
        "cross": lambda n, piece: cross(rb, wide, crossed, len(STAGES[n]), piece * 20, 40) if piece % 2 == 0 and piece < 4 else None,
        "lags": lags,
        "relay": lambda n: reduces[n].relay(),
        "after_x": lambda n: reduces[n].combine_x(),
        "after_y": lambda n: reduces[n].combine_y(),
        "final": lambda s: reduces[s].final(stacked),
    }
    for name, *arguments in PROGRAM:
        run[name](*arguments)
    out[...] = stacked[: LAGS * VS, :].astype(jnp.bfloat16)
    for gather in gathers:
        gather.drain()
    for reduce in reduces:
        reduce.drain()


def hand_on(source, target):
    target[...] = source[...]


def per_device(spectra, pattern, slot_of_pair, table):
    vmem = pl.BlockSpec(memory_space=pltpu.VMEM)
    smem = pl.BlockSpec(memory_space=pltpu.SMEM)
    hbm = pl.BlockSpec(memory_space=pl.ANY)
    stacks = pl.pallas_call(
        kernel,
        out_shape=jax.ShapeDtypeStruct((LAGS * VS, 128), jnp.bfloat16),
        in_specs=[hbm, hbm, smem, smem],
        out_specs=vmem,
        scratch_shapes=[
            pltpu.VMEM((NG, 256, 128), jnp.bfloat16),
            pltpu.VMEM((2, 2, 2 * 128, 128), jnp.float32),
            pltpu.VMEM((MOST, 2, SLOTS, NG, 128), jnp.float32),
            pltpu.VMEM((SLOTS, 2 * F, 128 * MOST), jnp.bfloat16),
            pltpu.VMEM((2, WINDOWS // 8, F, 128), jnp.bfloat16),
            pltpu.VMEM((LAGS, 2 * F), jnp.bfloat16),
            pltpu.VMEM((LAGS * VS + 8, 128), jnp.float32),
            pltpu.SemaphoreType.DMA((6,)),
            pltpu.VMEM((VS, 2, YS, LAGS, 128), jnp.bfloat16),
            pltpu.VMEM((VS, YS, FIRST, 128), jnp.bfloat16),
            pltpu.VMEM((VS, YS - 1, FIRST, 128), jnp.bfloat16),
            pltpu.VMEM((VS, 2, 2, 2, HALF, 128), jnp.bfloat16),
            pltpu.VMEM((VS, REST, 128), jnp.bfloat16),
            pltpu.VMEM((VS, REST, 128), jnp.bfloat16),
            pltpu.VMEM((VS, 2, 2, HALF, 128), jnp.bfloat16),
            pltpu.SemaphoreType.DMA((len(STAGES), 3)),
            pltpu.SemaphoreType.DMA((len(STAGES), 16)),
            pltpu.SemaphoreType.DMA((len(STAGES), 5)),
            pltpu.SemaphoreType.DMA((len(STAGES), 5)),
                ]
        + [pltpu.VMEM((4 * ZS, len(stage), NG, 256), jnp.bfloat16) for stage in STAGES],
        compiler_params=pltpu.CompilerParams(collective_id=0, has_side_effects=True, vmem_limit_bytes=56 << 20),
        name="correlate",
    )(spectra, table, pattern, slot_of_pair)
    stacks = pl.pallas_call(
        hand_on,
        out_shape=jax.ShapeDtypeStruct(stacks.shape, stacks.dtype),
        in_specs=[vmem],
        out_specs=vmem,
        name="hand_on",
    )(stacks)
    return stacks.reshape(1, LAGS, VS, 128)


def solution(mesh):
    mapped = jax.shard_map(
        per_device,
        mesh=mesh,
        in_specs=(P(None, "grp", None, "blk"), P(), P(), P()),
        out_specs=P("grp", None, None, "blk"),
        check_vma=False,
    )
    return lambda spectra, pattern, slot_of_pair: mapped(spectra, pattern, slot_of_pair, jnp.asarray(lag_rows()))
```
